32 devices in a mesh: gx: 2 (over y), gy: 4 (over x, core), gz: 4 (over z).
Axes of the slice: x: 2, y: 2, z: 4, core: 2. Of those that a mesh axis runs over, the one named last changes fastest.
Arguments:
- node_feat: float32 [16384, 128], P(('gx', 'gy', 'gz')), may hold values from -6 to 6
- edge_feat: float32 [65536, 128], P(('gx', 'gy', 'gz')), may hold values from -6 to 6
- node_cot: float32 [16384, 128], P(('gx', 'gy', 'gz')), may hold values from -6 to 6
- edge_cot: float32 [65536, 128], P(('gx', 'gy', 'gz')), may hold values from -6 to 6
- sender: int32 [65536], P(('gx', 'gy', 'gz')), may hold values from 0 to 1375, as said below
- receiver: int32 [65536], P(('gx', 'gy', 'gz')), may hold values from 0 to 511, as said below
- block_count: int32 [512], P(('gx', 'gy', 'gz')), may hold values from 0 to 128, as said below
- send_rows: int32 [6, 12, 12, 32], P('gx', 'gy', 'gz'), may hold values from 0 to 511, as said below
- edge_in_weight: float32 [384, 128], replicated, may hold values from -0.3125 to 0.3125
- edge_bias: float32 [128], replicated, may hold values from -3 to 3
- edge_out_weight: float32 [128, 128], replicated, may hold values from -0.5 to 0.5
- edge_gain: float32 [128], replicated, may hold values from 0.1 to 1.9
- node_in_weight: float32 [256, 128], replicated, may hold values from -0.375 to 0.375
- node_bias: float32 [128], replicated, may hold values from -3 to 3
- node_out_weight: float32 [128, 128], replicated, may hold values from -0.5 to 0.5
- node_gain: float32 [128], replicated, may hold values from 0.1 to 1.9
Outputs:
- node_grad: float32 [16384, 128], P(('gx', 'gy', 'gz'))
- edge_grad: float32 [65536, 128], P(('gx', 'gy', 'gz'))
- edge_in_grad: float32 [384, 128], replicated
- edge_bias_grad: float32 [128], replicated
- edge_out_grad: float32 [128, 128], replicated
- edge_gain_grad: float32 [128], replicated
- node_in_grad: float32 [256, 128], replicated
- node_bias_grad: float32 [128], replicated
- node_out_grad: float32 [128, 128], replicated
- node_gain_grad: float32 [128], replicated
The draws below stay inside these ranges and needn't reach their ends.
Inputs may be any that keep to these rules, and one draw needn't show every extreme that they name: `sender`: A value below 512 is an owned cell; otherwise it is 512 + 32 index(d) + s with s below 32, a halo slot of direction d. It never names direction 13 nor a direction whose neighbour lies outside the device grid. `receiver`: nondecreasing over the edge rows of one device. `block_count`: the nonzero blocks of a device come first; some device has no empty block. `send_rows`: the 32 cells of one list are distinct.
All inputs are finite; a program needn't handle non-finite values.
Results may differ from the reference program's by a relative error of at most 0.000088.
Values sent between devices are 32-bit elements; how exact they have to be, the bound alone decides.
A program may use at most 64 MiB of HBM per device.

```python
import math
import jax
import jax.numpy as jnp
from jax import lax

HID = 128
CELLS = 512
EDGES_DEV = 2048
BLOCKS = 16
SLOT = 32
GRID_X = 2
GRID_Y = 4
GRID_Z = 4
NODES = 16384
EDGES = 65536
DEVICES = 32


def draw_sender(key, part):
    key = jax.random.fold_in(key, 11)
    pick_key, remote_key, place_key, home_key = jax.random.split(key, 4)
    total = DEVICES * EDGES_DEV
    device = jnp.arange(total, dtype=jnp.int32) // EDGES_DEV
    coord_x = device // (GRID_Y * GRID_Z)
    coord_y = device // GRID_Z % GRID_Y
    coord_z = device % GRID_Z
    direction = jax.random.randint(pick_key, (total,), 0, 27, dtype=jnp.int32)
    step_x = direction // 9 - 1
    step_y = direction // 3 % 3 - 1
    step_z = direction % 3 - 1
    inside = (coord_x + step_x >= 0) & (coord_x + step_x < GRID_X)
    inside = inside & (coord_y + step_y >= 0) & (coord_y + step_y < GRID_Y)
    inside = inside & (coord_z + step_z >= 0) & (coord_z + step_z < GRID_Z) & (direction != 13)
    remote = jax.random.randint(remote_key, (total,), 0, 2, dtype=jnp.int32) < 1
    position = jax.random.randint(place_key, (total,), 0, SLOT, dtype=jnp.int32)
    local_row = jax.random.randint(home_key, (total,), 0, CELLS, dtype=jnp.int32)
    halo_row = CELLS + direction * SLOT + position
    return jnp.where(remote & inside, halo_row, local_row).astype(jnp.int32)


def draw_receiver(key, part):
    key = jax.random.fold_in(key, 12)
    raw_rows = jax.random.randint(key, (DEVICES, EDGES_DEV), 0, CELLS, dtype=jnp.int32)
    return jnp.sort(raw_rows, axis=1).reshape(DEVICES * EDGES_DEV)


def draw_block_count(key, part):
    key = jax.random.fold_in(key, 13)
    live_key, fill_key, top_key, device_key = jax.random.split(key, 4)
    live = jax.random.randint(live_key, (DEVICES, 1), max(1, BLOCKS // 8), BLOCKS + 1, dtype=jnp.int32)
    device_index = jnp.arange(DEVICES, dtype=jnp.int32)[:, None]
    full_device = jax.random.randint(device_key, (), 0, DEVICES, dtype=jnp.int32)
    live = jnp.where(device_index == full_device, BLOCKS, live)
    fill = jax.random.randint(fill_key, (DEVICES, BLOCKS), 64, 129, dtype=jnp.int32)
    top_block = jax.random.randint(top_key, (), 0, BLOCKS, dtype=jnp.int32)
    block_index = jnp.arange(BLOCKS, dtype=jnp.int32)[None, :]
    fill = jnp.where((block_index == top_block) & (device_index == full_device), 128, fill)
    return jnp.where(block_index < live, fill, 0).astype(jnp.int32).reshape(DEVICES * BLOCKS)


def draw_send_rows(key, part):
    key = jax.random.fold_in(key, 14)
    list_keys = jax.random.split(key, DEVICES * 27)
    rows = jax.vmap(lambda single: jax.random.permutation(single, CELLS)[:SLOT])(list_keys).astype(jnp.int32)
    rows = rows.reshape(GRID_X, GRID_Y, GRID_Z, 3, 3, 3, SLOT).transpose(0, 3, 1, 4, 2, 5, 6)
    return rows.reshape(3 * GRID_X, 3 * GRID_Y, 3 * GRID_Z, SLOT)


def levels(own_key, shape, cuts, least, high):
    factor_of = 1.0
    for dim, shards_of in cuts:
        steps = jax.random.uniform(jax.random.fold_in(jax.random.fold_in(own_key, 6), dim), (shards_of,), jnp.float32, least / len(cuts), high / len(cuts))
        factor_of = factor_of * jnp.repeat(jnp.exp(steps), shape[dim] // shards_of).reshape((-1,) + (1,) * (len(shape) - 1 - dim))
    return factor_of


def bell_draw(own_key, extent, deviation, limit, cuts=(), kind=jnp.bfloat16):
    entries = deviation * jax.random.normal(own_key, extent, jnp.float32)
    if cuts:
        entries = entries * levels(own_key, extent, cuts, -0.22, 0.18)
    return jnp.clip(entries, -limit, limit).astype(kind)


def setup_inputs(seed: int = 0) -> dict:
    keys = jax.random.split(jax.random.key(seed), 17)
    node_feat = bell_draw(keys[0], (NODES, HID), 1.0, 6.0, ((0, 32),), jnp.float32)
    edge_feat = bell_draw(keys[1], (EDGES, HID), 1.0, 6.0, ((0, 32),), jnp.float32)
    node_cot = bell_draw(keys[2], (NODES, HID), 1.0, 6.0, ((0, 32),), jnp.float32)
    edge_cot = bell_draw(keys[3], (EDGES, HID), 1.0, 6.0, ((0, 32),), jnp.float32)
    sender = draw_sender(jax.random.fold_in(keys[16], 71), 0)
    receiver = draw_receiver(jax.random.fold_in(keys[16], 71), 0)
    block_count = draw_block_count(jax.random.fold_in(keys[16], 71), 0)
    send_rows = draw_send_rows(jax.random.fold_in(keys[16], 71), 0)
    edge_in_weight = bell_draw(keys[8], (3 * HID, HID), (3 * HID) ** -0.5, 0.3125, (), jnp.float32)
    edge_bias = bell_draw(keys[9], (HID,), 0.5, 3.0, (), jnp.float32)
    edge_out_weight = bell_draw(keys[10], (HID, HID), HID ** -0.5, 0.5, (), jnp.float32)
    edge_gain = jnp.clip(1.0 + 0.18 * jax.random.normal(keys[11], (HID,), jnp.float32), 0.1, 1.9)
    node_in_weight = bell_draw(keys[12], (2 * HID, HID), (2 * HID) ** -0.5, 0.375, (), jnp.float32)
    node_bias = bell_draw(keys[13], (HID,), 0.5, 3.0, (), jnp.float32)
    node_out_weight = bell_draw(keys[14], (HID, HID), HID ** -0.5, 0.5, (), jnp.float32)
    node_gain = jnp.clip(1.0 + 0.18 * jax.random.normal(keys[15], (HID,), jnp.float32), 0.1, 1.9)
    return {"node_feat": node_feat, "edge_feat": edge_feat, "node_cot": node_cot, "edge_cot": edge_cot, "sender": sender, "receiver": receiver, "block_count": block_count, "send_rows": send_rows, "edge_in_weight": edge_in_weight, "edge_bias": edge_bias, "edge_out_weight": edge_out_weight, "edge_gain": edge_gain, "node_in_weight": node_in_weight, "node_bias": node_bias, "node_out_weight": node_out_weight, "node_gain": node_gain}


NORM_EPS = 1e-05
HIGHEST = lax.Precision.HIGHEST

def layer_norm(values, gain):
    average = lax.optimization_barrier(jnp.mean(values, axis=-1, keepdims=True))
    centred = values - average
    spread_sq = lax.optimization_barrier(jnp.mean(centred * centred, axis=-1, keepdims=True))
    return centred * lax.rsqrt(spread_sq + NORM_EPS) * gain

def edge_section(node_table, edge_feat, sender, receiver, valid_mask, edge_in_weight, edge_bias, edge_out_weight, edge_gain):
    width = edge_feat.shape[1]
    preact = jnp.dot(edge_feat, edge_in_weight[:width], precision=HIGHEST)
    preact = preact + jnp.dot(node_table[sender], edge_in_weight[width:2 * width], precision=HIGHEST)
    preact = preact + jnp.dot(node_table[receiver], edge_in_weight[2 * width:], precision=HIGHEST)
    hidden = jax.nn.silu(preact + edge_bias)
    return layer_norm(jnp.dot(hidden, edge_out_weight, precision=HIGHEST), edge_gain) * valid_mask[:, None]

def node_section(node_feat, summed, node_in_weight, node_bias, node_out_weight, node_gain):
    width = node_feat.shape[1]
    preact = jnp.dot(node_feat, node_in_weight[:width], precision=HIGHEST) + jnp.dot(summed, node_in_weight[width:], precision=HIGHEST)
    hidden = jax.nn.silu(preact + node_bias)
    return node_feat + layer_norm(jnp.dot(hidden, node_out_weight, precision=HIGHEST), node_gain)

def from_neighbours(packets):
    grid_x, grid_y, grid_z = (packets.shape[0], packets.shape[1], packets.shape[2])
    padded = jnp.pad(packets, ((1, 1), (1, 1), (1, 1), (0, 0), (0, 0), (0, 0), (0, 0), (0, 0)))
    pieces = []
    for direction in range(27):
        step_x = direction // 9 - 1
        step_y = direction // 3 % 3 - 1
        step_z = direction % 3 - 1
        pieces.append(padded[1 + step_x:1 + step_x + grid_x, 1 + step_y:1 + step_y + grid_y, 1 + step_z:1 + step_z + grid_z, 1 - step_x, 1 - step_y, 1 - step_z])
    stacked = jnp.stack(pieces, axis=3)
    return stacked.reshape(grid_x, grid_y, grid_z, 3, 3, 3, packets.shape[6], packets.shape[7])

def device_backward(item, weights):
    node_feat, received, edge_feat, node_cot, edge_cot, sender, receiver, valid_mask = item
    edge_in_weight, edge_bias, edge_out_weight, edge_gain, node_in_weight, node_bias, node_out_weight, node_gain = weights
    num_cells = node_feat.shape[0]
    node_table = jnp.concatenate([node_feat, received], axis=0)

    def edge_part(table_in, feat_in, weight_in, bias_in, weight_out, gain_in):
        return edge_section(table_in, feat_in, sender, receiver, valid_mask, weight_in, bias_in, weight_out, gain_in)
    message, edge_pull = jax.vjp(edge_part, node_table, edge_feat, edge_in_weight, edge_bias, edge_out_weight, edge_gain)
    summed = jax.ops.segment_sum(message, receiver, num_segments=num_cells, indices_are_sorted=True)
    _, node_pull = jax.vjp(node_section, node_feat, summed, node_in_weight, node_bias, node_out_weight, node_gain)
    node_grads = node_pull(node_cot)
    edge_grads = edge_pull(edge_cot + node_grads[1][receiver])
    table_grad = edge_grads[0]
    own_grad = node_grads[0] + table_grad[:num_cells]
    grads = (edge_grads[2], edge_grads[3], edge_grads[4], edge_grads[5], node_grads[2], node_grads[3], node_grads[4], node_grads[5])
    return (own_grad, table_grad[num_cells:], edge_cot + edge_grads[1], grads)

def reference(node_feat, edge_feat, node_cot, edge_cot, sender, receiver, block_count, send_rows, edge_in_weight, edge_bias, edge_out_weight, edge_gain, node_in_weight, node_bias, node_out_weight, node_gain):
    outer_mask = (jnp.arange(27) != 13).astype(jnp.float32).reshape(3, 3, 3, 1, 1)
    node_blocks = node_feat.reshape(GRID_X, GRID_Y, GRID_Z, CELLS, HID)
    row_lists = send_rows.reshape(GRID_X, 3, GRID_Y, 3, GRID_Z, 3, SLOT).transpose(0, 2, 4, 1, 3, 5, 6)
    packets = jax.vmap(jax.vmap(jax.vmap(lambda block, rows: block[rows])))(node_blocks, row_lists) * outer_mask
    received = from_neighbours(packets)
    valid_mask = (lax.broadcasted_iota(jnp.int32, (DEVICES * BLOCKS, 128), 1) < block_count[:, None]).astype(jnp.float32)
    weights = (edge_in_weight, edge_bias, edge_out_weight, edge_gain, node_in_weight, node_bias, node_out_weight, node_gain)
    items = (node_feat.reshape(DEVICES, CELLS, HID), received.reshape(DEVICES, 27 * SLOT, HID), edge_feat.reshape(DEVICES, EDGES_DEV, HID), node_cot.reshape(DEVICES, CELLS, HID), edge_cot.reshape(DEVICES, EDGES_DEV, HID), sender.reshape(DEVICES, EDGES_DEV), receiver.reshape(DEVICES, EDGES_DEV), valid_mask.reshape(DEVICES, EDGES_DEV))
    own_grad, slot_grad, edge_grad, grads = lax.map(lambda item: device_backward(item, weights), items)
    slot_grad = slot_grad.reshape(GRID_X, GRID_Y, GRID_Z, 3, 3, 3, SLOT, HID) * outer_mask
    returned = from_neighbours(slot_grad) * outer_mask
    base_rows = jnp.arange(DEVICES, dtype=jnp.int32).reshape(GRID_X, GRID_Y, GRID_Z, 1, 1, 1, 1) * CELLS
    flat_rows = (base_rows + row_lists).reshape(-1)
    node_grad = own_grad.reshape(NODES, HID) + jax.ops.segment_sum(returned.reshape(-1, HID), flat_rows, num_segments=NODES)
    grad_scale = 1.0 / math.sqrt(DEVICES * EDGES_DEV)
    summed_grads = [lax.optimization_barrier(jnp.sum(entry, axis=0)) * grad_scale for entry in grads]
    return (node_grad, edge_grad.reshape(EDGES, HID), summed_grads[0], summed_grads[1], summed_grads[2], summed_grads[3], summed_grads[4], summed_grads[5], summed_grads[6], summed_grads[7])
```

```python
import functools
import math

import jax
import jax.numpy as jnp
from jax import lax
from jax.experimental import pallas as pl
from jax.experimental.pallas import tpu as pltpu
from jax.sharding import PartitionSpec as P

NORM_EPS = 1e-05
LANES = 128
CHUNK = 512
AXES = ("gx", "gy", "gz")
F32, BF16 = jnp.float32, jnp.bfloat16
VMEM = pl.BlockSpec(memory_space=pltpu.VMEM)


def split(x):
    high = x.astype(BF16)
    low = (x - high.astype(F32)).astype(BF16)
    return jnp.concatenate([high, low], axis=1)


def dense(w):
    row = split(w)
    return jnp.concatenate([row, row], axis=0)


def halves(y):
    return y[:, :LANES] + y[:, LANES:]


def mul(a, b):
    return jnp.dot(a, b, preferred_element_type=F32)


def mul_t(a, b):
    y = lax.dot_general(a, b, (((0,), (0,)), ((), ())), preferred_element_type=F32)
    return halves(y[:LANES] + y[LANES:])


def hot(mask):
    return jnp.where(mask, 1.0, 0.0).astype(BF16)


def pick_rows(idx_row, blocks):
    col = jnp.broadcast_to(idx_row, (LANES, LANES)).T
    lane = lax.broadcasted_iota(jnp.int32, (LANES, LANES), 1)
    return jnp.concatenate([hot(col == lane + LANES * k) for k in range(blocks)], axis=1)


def pick_cols(idx_ref, tile, blocks):
    row = lax.broadcasted_iota(jnp.int32, (LANES, LANES), 0) + LANES * tile
    return jnp.concatenate(
        [hot(jnp.broadcast_to(idx_ref[b : b + 1, :], (LANES, LANES)) == row) for b in range(blocks)],
        axis=1,
    )


def centre(x):
    return x - jnp.mean(x, axis=-1, keepdims=True)


def pack_kernel(feat_ref, rows_ref, out_ref):
    table = split(feat_ref[...])
    cells = feat_ref.shape[0]
    for b in range(rows_ref.shape[0]):
        one = pick_rows(rows_ref[b : b + 1, :], cells // LANES)
        out_ref[b * LANES : (b + 1) * LANES, :] = halves(mul(one, table))


def collect_kernel(own_ref, back_ref, rows_ref, out_ref):
    grads = split(back_ref[...])
    for t in range(own_ref.shape[0] // LANES):
        at = slice(t * LANES, (t + 1) * LANES)
        out_ref[at, :] = own_ref[at, :] + halves(mul(pick_cols(rows_ref, t, rows_ref.shape[0]), grads))


def layer_kernel(
    scale,
    feat_ref, halo_ref, edge_ref, ncot_ref, ecot_ref, snd_ref, rcv_ref, cnt_ref,
    ein_ref, ebias_ref, eout_ref, egain_ref, nin_ref, nbias_ref, nout_ref, ngain_ref,
    own_ref, slot_ref, egrad_ref, wgrad_ref,
    table, both, edge_hl, hid_hl, dsilu_s, xhat_s, rstd_s, msg_hl, dout_hl, dpre_hl, up_s, recv_s,
):
    cells, halo = feat_ref.shape[0], halo_ref.shape[0]
    edges = edge_ref.shape[0]
    tbl = cells + halo
    sub = CHUNK // LANES
    eblocks = edges // LANES
    ein = ein_ref[...]
    w_e, w_s, w_r = ein[:LANES], ein[LANES : 2 * LANES], ein[2 * LANES :]
    eoc = centre(eout_ref[...])
    gain, bias = egain_ref[...], ebias_ref[...]

    table[:cells, :] = split(feat_ref[...])
    table[cells:, :] = split(halo_ref[...])
    both[:tbl, :] = split(halves(mul(table[...], dense(w_s))))
    both[tbl:, :] = split(halves(mul(table[:cells, :], dense(w_r))))
    we_cat, wo_cat = dense(w_e), dense(eoc)

    def valid_of(c):
        row = lax.broadcasted_iota(jnp.int32, (LANES, LANES), 0)
        return jnp.concatenate([jnp.where(row < cnt_ref[c * sub + k], 1.0, 0.0) for k in range(sub)], axis=0)

    def rcv_rows(c):
        return jnp.concatenate(
            [pick_rows(rcv_ref[pl.ds(c * sub + k, 1), :], cells // LANES) for k in range(sub)], axis=0
        )

    def forward(c, carry):
        at = pl.ds(pl.multiple_of(c * CHUNK, CHUNK), CHUNK)
        one = jnp.concatenate(
            [pick_rows(snd_ref[pl.ds(c * sub + k, 1), :], tbl // LANES) for k in range(sub)], axis=0
        )
        one = jnp.concatenate([one, rcv_rows(c)], axis=1)
        feat = split(edge_ref[at, :])
        edge_hl[at, :] = feat
        pre = halves(mul(one, both[...]) + mul(feat, we_cat)) + bias
        sig = jax.nn.sigmoid(pre)
        hid = pre * sig
        dsilu_s[at, :] = sig + hid * (1.0 - sig)
        hid = split(hid)
        hid_hl[at, :] = hid
        out = halves(mul(hid, wo_cat))
        rstd = lax.rsqrt(jnp.mean(out * out, axis=-1, keepdims=True) + NORM_EPS)
        xhat = out * rstd
        rstd_s[at, :] = jnp.broadcast_to(rstd, out.shape)
        xhat_s[at, :] = xhat
        msg_hl[at, :] = split(xhat * gain * valid_of(c))
        return carry

    lax.fori_loop(0, edges // CHUNK, forward, 0)

    summed = jnp.concatenate(
        [halves(mul(pick_cols(rcv_ref, t, eblocks), msg_hl[...])) for t in range(cells // LANES)], axis=0
    )
    nin, ngain = nin_ref[...], ngain_ref[...]
    noc = centre(nout_ref[...])
    feat_hl, sum_hl = table[:cells, :], split(summed)
    pre = halves(mul(feat_hl, dense(nin[:LANES])) + mul(sum_hl, dense(nin[LANES:]))) + nbias_ref[...]
    sig = jax.nn.sigmoid(pre)
    hid = pre * sig
    dsilu = sig + hid * (1.0 - sig)
    hid = split(hid)
    out = halves(mul(hid, dense(noc)))
    rstd = lax.rsqrt(jnp.mean(out * out, axis=-1, keepdims=True) + NORM_EPS)
    xhat = out * rstd
    ncot = ncot_ref[...]
    dn = ncot * ngain
    dout = split(rstd * (dn - xhat * jnp.mean(dn * xhat, axis=-1, keepdims=True)))
    dpre = halves(mul(dout, dense(noc.T))) * dsilu
    dpre_n = split(dpre)
    own_ref[...] = ncot + halves(mul(dpre_n, dense(nin[:LANES].T)))
    dsum = split(halves(mul(dpre_n, dense(nin[LANES:].T))))
    wgrad_ref[512:640, :] = mul_t(feat_hl, dpre_n) * scale
    wgrad_ref[640:768, :] = mul_t(sum_hl, dpre_n) * scale
    wgrad_ref[768:896, :] = centre(mul_t(hid, dout)) * scale
    nbias_g = jnp.sum(dpre, axis=0, keepdims=True)
    ngain_g = jnp.sum(ncot * xhat, axis=0, keepdims=True)

    wot_cat, wet_cat = dense(eoc.T), dense(w_e.T)

    def backward(c, carry):
        bias_g, gain_g = carry
        at = pl.ds(pl.multiple_of(c * CHUNK, CHUNK), CHUNK)
        ecot = ecot_ref[at, :]
        xhat = xhat_s[at, :]
        dm = (ecot + halves(mul(rcv_rows(c), dsum))) * valid_of(c)
        dn = dm * gain
        dout = split(rstd_s[at, :] * (dn - xhat * jnp.mean(dn * xhat, axis=-1, keepdims=True)))
        dout_hl[at, :] = dout
        dpre = halves(mul(dout, wot_cat)) * dsilu_s[at, :]
        dpre_c = split(dpre)
        dpre_hl[at, :] = dpre_c
        egrad_ref[at, :] = ecot + halves(mul(dpre_c, wet_cat))
        fold = lambda x: jnp.sum(x.reshape(CHUNK // 8, 8, LANES), axis=0)
        return bias_g + fold(dpre), gain_g + fold(dm * xhat)

    zero = jnp.zeros((8, LANES), F32)
    ebias_g, egain_g = lax.fori_loop(0, edges // CHUNK, backward, (zero, zero))

    wgrad_ref[384:512, :] = centre(mul_t(hid_hl[...], dout_hl[...])) * scale
    wgrad_ref[0:128, :] = mul_t(edge_hl[...], dpre_hl[...]) * scale
    wgrad_ref[896:904, :] = jnp.concatenate(
        [
            jnp.sum(ebias_g, axis=0, keepdims=True),
            jnp.sum(egain_g, axis=0, keepdims=True),
            nbias_g,
            ngain_g,
            jnp.zeros((4, LANES), F32),
        ],
        axis=0,
    ) * scale

    def up(t, carry):
        out = pl.ds(pl.multiple_of(t * LANES, LANES), LANES)
        up_s[out, :] = split(halves(mul(pick_cols(snd_ref, t, eblocks), dpre_hl[...])))
        return carry

    lax.fori_loop(0, tbl // LANES, up, 0)

    def down(t, carry):
        out = pl.ds(pl.multiple_of(t * LANES, LANES), LANES)
        recv_s[out, :] = split(halves(mul(pick_cols(rcv_ref, t, eblocks), dpre_hl[...])))
        return carry

    lax.fori_loop(0, cells // LANES, down, 0)

    wst = dense(w_s.T)
    own_ref[...] += halves(mul(up_s[:cells, :], wst) + mul(recv_s[...], dense(w_r.T)))
    slot_ref[...] = halves(mul(up_s[cells:, :], wst))
    wgrad_ref[128:256, :] = mul_t(table[...], up_s[...]) * scale
    wgrad_ref[256:384, :] = mul_t(table[:cells, :], recv_s[...]) * scale


def swap(value):
    for dim, axis in enumerate(AXES):
        peers = lax.axis_size(axis)
        up = [(i, i + 1) for i in range(peers - 1)]
        down = [(j, i) for i, j in up]
        low = lax.slice_in_dim(value, 0, 1, axis=dim)
        mid = lax.slice_in_dim(value, 1, 2, axis=dim)
        high = lax.slice_in_dim(value, 2, 3, axis=dim)
        before = lax.ppermute(high, axis, up)
        after = lax.ppermute(low, axis, down)
        value = jnp.concatenate([before, mid, after], axis=dim)
    return value


def on_device(
    node_feat, edge_feat, node_cot, edge_cot, sender, receiver, block_count, send_rows,
    edge_in_weight, edge_bias, edge_out_weight, edge_gain,
    node_in_weight, node_bias, node_out_weight, node_gain,
):
    cells, width = node_feat.shape
    edges = edge_feat.shape[0]
    slots = send_rows.shape[3]
    total = lax.axis_size("gx") * lax.axis_size("gy") * lax.axis_size("gz") * edges
    scale = 1.0 / math.sqrt(total)
    halo = -(-27 * slots // LANES) * LANES
    rows = jnp.where((jnp.arange(27) != 13)[:, None], send_rows.reshape(27, slots), -1).reshape(27 * slots)
    rows = jnp.pad(rows, (0, halo - 27 * slots), constant_values=-1).reshape(halo // LANES, LANES)

    def exchange(x):
        y = swap(x[: 27 * slots].reshape(3, 3, 3, slots, width)).reshape(27 * slots, width)
        return jnp.pad(y, ((0, halo - 27 * slots), (0, 0)))

    packets = pl.pallas_call(
        pack_kernel, out_shape=jax.ShapeDtypeStruct((halo, width), F32), in_specs=[VMEM] * 2, out_specs=VMEM,
        name="pack",
    )(node_feat, rows)
    received = exchange(packets)
    tbl = cells + halo
    big = lambda dtype, cols: pltpu.VMEM((edges, cols), dtype)
    own, slot, edge_grad, wgrad = pl.pallas_call(
        functools.partial(layer_kernel, scale),
        out_shape=(
            jax.ShapeDtypeStruct((cells, width), F32),
            jax.ShapeDtypeStruct((halo, width), F32),
            jax.ShapeDtypeStruct((edges, width), F32),
            jax.ShapeDtypeStruct((904, width), F32),
        ),
        in_specs=[VMEM] * 7 + [pl.BlockSpec(memory_space=pltpu.SMEM)] + [VMEM] * 8,
        out_specs=(VMEM,) * 4,
        scratch_shapes=[
            pltpu.VMEM((tbl, 256), BF16),
            pltpu.VMEM((tbl + cells, 256), BF16),
            big(BF16, 256),
            big(BF16, 256),
            big(F32, 128),
            big(F32, 128),
            big(F32, 128),
            big(BF16, 256),
            big(BF16, 256),
            big(BF16, 256),
            pltpu.VMEM((tbl, 256), BF16),
            pltpu.VMEM((cells, 256), BF16),
        ],
        compiler_params=pltpu.CompilerParams(vmem_limit_bytes=48 * 1024 * 1024),
        name="layer",
    )(
        node_feat, received, edge_feat, node_cot, edge_cot,
        sender.reshape(edges // LANES, LANES), receiver.reshape(edges // LANES, LANES), block_count,
        edge_in_weight, edge_bias.reshape(1, width), edge_out_weight, edge_gain.reshape(1, width),
        node_in_weight, node_bias.reshape(1, width), node_out_weight, node_gain.reshape(1, width),
    )
    total_grad = lax.psum(wgrad, AXES)
    back = exchange(slot)
    node_grad = pl.pallas_call(
        collect_kernel, out_shape=jax.ShapeDtypeStruct((cells, width), F32), in_specs=[VMEM] * 3, out_specs=VMEM,
        name="collect",
    )(own, back, rows)
    return (
        node_grad, edge_grad,
        total_grad[0:384], total_grad[896], total_grad[384:512], total_grad[897],
        total_grad[512:768], total_grad[898], total_grad[768:896], total_grad[899],
    )


def solution(mesh):
    part = P(AXES, None)
    flat = P(AXES)
    return jax.shard_map(
        on_device,
        mesh=mesh,
        in_specs=(part,) * 4 + (flat,) * 3 + (P("gx", "gy", "gz", None),) + (P(),) * 8,
        out_specs=(part,) * 2 + (P(),) * 8,
        check_vma=False,
    )
```

```python
import functools
import math

import jax
import jax.numpy as jnp
from jax import lax
from jax.experimental import pallas as pl
from jax.experimental.pallas import tpu as pltpu
from jax.sharding import PartitionSpec as P

NORM_EPS = 1e-05
LANES = 128
CHUNK = 512
GRAD_ROWS = 1024
AXES = ("gx", "gy", "gz")
F32, BF16 = jnp.float32, jnp.bfloat16
VMEM = pl.BlockSpec(memory_space=pltpu.VMEM)


def split(x):
    high = x.astype(BF16)
    low = (x - high.astype(F32)).astype(BF16)
    return jnp.concatenate([high, low], axis=1)


def dense(w):
    row = split(w)
    return jnp.concatenate([row, row], axis=0)


def halves(y):
    return y[:, :LANES] + y[:, LANES:]


def mul(a, b):
    return jnp.dot(a, b, preferred_element_type=F32)


def mul_t(a, b):
    y = lax.dot_general(a, b, (((0,), (0,)), ((), ())), preferred_element_type=F32)
    return halves(y[:LANES] + y[LANES:])


def hot(mask):
    return jnp.where(mask, 1.0, 0.0).astype(BF16)


def pick_rows(idx_row, blocks):
    col = jnp.broadcast_to(idx_row, (LANES, LANES)).T
    lane = lax.broadcasted_iota(jnp.int32, (LANES, LANES), 1)
    return jnp.concatenate([hot(col == lane + LANES * k) for k in range(blocks)], axis=1)


def pick_cols(idx_ref, tile, blocks):
    row = lax.broadcasted_iota(jnp.int32, (LANES, LANES), 0) + LANES * tile
    return jnp.concatenate(
        [hot(jnp.broadcast_to(idx_ref[b : b + 1, :], (LANES, LANES)) == row) for b in range(blocks)],
        axis=1,
    )


def centre(x):
    return x - jnp.mean(x, axis=-1, keepdims=True)


def position(sizes):
    return tuple(lax.axis_index(axis) for axis in AXES), sizes


def directions(spot):
    at, sizes = spot
    for d in range(27):
        if d == 13:
            continue
        step = (d // 9 - 1, d // 3 % 3 - 1, d % 3 - 1)
        if any(n == 1 and s != 0 for n, s in zip(sizes, step)):
            continue
        inside = None
        for p, n, s in zip(at, sizes, step):
            if s:
                ok = p > 0 if s < 0 else p < n - 1
                inside = ok if inside is None else jnp.logical_and(inside, ok)
        yield d, inside, tuple(p + s for p, s in zip(at, step))


def greet_neighbours(spot, barrier):
    for _, inside, where in directions(spot):

        @pl.when(inside)
        def _():
            pl.semaphore_signal(barrier, inc=1, device_id=where, device_id_type=pl.DeviceIdType.MESH)

    count = 1
    for p, n in zip(*spot):
        count = count * (1 + (p > 0).astype(jnp.int32) + (p < n - 1).astype(jnp.int32))
    return count - 1


def halo_copy(d, where, out, land, send, recv):
    return pltpu.make_async_remote_copy(
        src_ref=out.at[d], dst_ref=land.at[26 - d], send_sem=send.at[d], recv_sem=recv.at[26 - d],
        device_id=where, device_id_type=pl.DeviceIdType.MESH,
    )


def halo_start(spot, out, land, send, recv):
    for d, inside, where in directions(spot):

        @pl.when(inside)
        def _():
            halo_copy(d, where, out, land, send, recv).start()


def halo_wait(spot, out, land, send, recv):
    for d, inside, where in directions(spot):

        @pl.when(inside)
        def _():
            halo_copy(d, where, out, land, send, recv).wait_send()
            halo_copy(26 - d, where, out, land, send, recv).wait_recv()


def pack_kernel(sizes, feat_ref, rows_ref, out_ref, packets, land, send, recv):
    spot = position(sizes)
    slots = packets.shape[1]
    land[...] = jnp.zeros_like(land)
    barrier = pltpu.get_barrier_semaphore()
    count = greet_neighbours(spot, barrier)
    table = split(feat_ref[...])
    cells = feat_ref.shape[0]
    for b in range(rows_ref.shape[0]):
        one = pick_rows(rows_ref[b : b + 1, :], cells // LANES)
        picked = halves(mul(one, table))
        for k in range(LANES // slots):
            d = b * (LANES // slots) + k
            if d < 27:
                packets[d] = picked[k * slots : (k + 1) * slots]
    pl.semaphore_wait(barrier, count)
    halo_start(spot, packets, land, send, recv)
    halo_wait(spot, packets, land, send, recv)
    out_ref[: 27 * slots, :] = land[...].reshape(27 * slots, LANES)
    out_ref[27 * slots :, :] = jnp.zeros((out_ref.shape[0] - 27 * slots, LANES), F32)


def factors(axis, size, whole):
    out, stride = [], 1
    if whole and size <= 4:
        return [(axis, 1, size)] if size > 1 else []
    while size % 2 == 0:
        out.append((axis, stride, 2))
        stride, size = 2 * stride, size // 2
    if size > 1:
        out.append((axis, stride, size))
    return out


def sum_plan(sizes, rows):
    fx, fy, fz = factors(0, sizes[0], False), factors(1, sizes[1], False), factors(2, sizes[2], True)
    slot = sem = 0
    plans = []

    def lay(steps, r):
        nonlocal slot, sem
        laid = []
        for axis, stride, n in steps:
            scatters = r % (8 * n) == 0
            r = r // n if scatters else r
            laid.append((axis, stride, n, scatters, r, slot, sem))
            slot, sem = slot + (n - 1) * r, sem + 2 * (n - 1)
        return laid, r

    common, r = lay(fy[:1], rows)
    part_a, end_a = lay(fy[1:] + fx + fz, r // 2)
    part_b, end_b = lay(fx + fy[1:] + fz, r // 2)
    return common, r, (part_a, end_a), (part_b, end_b), slot, sem


def sum_kernel(sizes, plan, part_ref, slot_ref, total_ref, back_ref, acc, full, rbuf, packets, land, send, recv, sems, rsems):
    spot = position(sizes)
    at = spot[0]
    common, r_common, (part_a, end_a), (part_b, end_b), _, _ = plan
    slots = packets.shape[1]

    def peer(step, k):
        axis, stride, n = step[:3]
        digit = lax.rem(at[axis] // stride, n)
        other = lax.rem(digit + k, n)
        where = list(at)
        where[axis] = at[axis] + (other - digit) * stride
        return digit, other, tuple(where)

    land[...] = jnp.zeros_like(land)
    barrier = pltpu.get_barrier_semaphore()
    count = greet_neighbours(spot, barrier)
    for step in common + part_a:
        for k in range(1, step[2]):
            pl.semaphore_signal(
                barrier, inc=1, device_id=peer(step, k)[2], device_id_type=pl.DeviceIdType.MESH
            )
            count = count + 1
    acc[...] = part_ref[...]
    for d in range(27):
        packets[d] = slot_ref[d * slots : (d + 1) * slots, :]
    pl.semaphore_wait(barrier, count)

    def block(ref, start, r):
        return ref.at[pl.ds(pl.multiple_of(start, 8), r)]

    def remote(src, dst, sem, where):
        return pltpu.make_async_remote_copy(
            src_ref=src, dst_ref=dst, send_sem=sems.at[sem], recv_sem=rsems.at[sem],
            device_id=where, device_id_type=pl.DeviceIdType.MESH,
        )

    def scatter(step, off, begin):
        _, _, n, scatters, r, slot, sem = step
        digit = None
        for k in range(1, n):
            digit, other, where = peer(step, k)
            src = block(acc, off + other * r if scatters else off, r)
            copy = remote(src, rbuf.at[pl.ds(slot + (k - 1) * r, r)], sem + k - 1, where)
            copy.start() if begin else copy.wait()
        mine = off + digit * r if scatters else off
        if begin:
            return mine
        here = pl.ds(pl.multiple_of(mine, 8), r)
        total = acc[here, :]
        for k in range(1, n):
            total = total + rbuf[slot + (k - 1) * r : slot + k * r, :]
        acc[here, :] = total
        return mine

    def gather(step, off, begin):
        _, _, n, scatters, r, slot, sem = step
        if not scatters:
            return off
        base = off
        for k in range(1, n):
            digit, other, where = peer(step, k)
            base = off - digit * r
            copy = remote(block(full, off, r), block(full, off, r), sem + n - 1 + k - 1, where)
            if begin:
                copy.start()
            else:
                copy.wait_send()
                source = lax.rem(digit - k + n, n)
                came = block(full, base + source * r, r)
                remote(came, came, sem + n - 1 + k - 1, where).wait_recv()
        return base

    off = 0
    for step in common:
        scatter(step, off, True)
    halo_start(spot, packets, land, send, recv)
    for step in common:
        off = scatter(step, off, False)
    starts = [off, off + r_common // 2]
    parts = [part_a, part_b]
    for i in range(len(part_a)):
        for j in range(2):
            if i:
                starts[j] = scatter(parts[j][i - 1], starts[j], False)
            scatter(parts[j][i], starts[j], True)
    for j, end in ((0, end_a), (1, end_b)):
        starts[j] = scatter(parts[j][-1], starts[j], False)
        here = pl.ds(pl.multiple_of(starts[j], 8), end)
        full[here, :] = acc[here, :]
        gather(parts[j][-1], starts[j], True)
    for i in reversed(range(len(part_a))):
        for j in range(2):
            starts[j] = gather(parts[j][i], starts[j], False)
            if i:
                gather(parts[j][i - 1], starts[j], True)
    off = starts[0]
    for step in reversed(common):
        copy_off = off
        grown = (step[0], step[1], step[2], step[3], step[4], step[5], step[6])
        gather(grown, copy_off, True)
        off = gather(grown, copy_off, False)
    halo_wait(spot, packets, land, send, recv)
    total_ref[...] = full[...]
    back_ref[: 27 * slots, :] = land[...].reshape(27 * slots, LANES)
    back_ref[27 * slots :, :] = jnp.zeros((back_ref.shape[0] - 27 * slots, LANES), F32)


def finish_kernel(
    own_ref, back_ref, rows_ref, total_ref,
    out_ref, ein_ref, ebias_ref, eout_ref, egain_ref, nin_ref, nbias_ref, nout_ref, ngain_ref,
):
    grads = split(back_ref[...])
    for t in range(own_ref.shape[0] // LANES):
        at = slice(t * LANES, (t + 1) * LANES)
        out_ref[at, :] = own_ref[at, :] + halves(mul(pick_cols(rows_ref, t, rows_ref.shape[0]), grads))
    ein_ref[...] = total_ref[0:384, :]
    eout_ref[...] = total_ref[384:512, :]
    nin_ref[...] = total_ref[512:768, :]
    nout_ref[...] = total_ref[768:896, :]
    ebias_ref[...] = total_ref[896:897, :]
    egain_ref[...] = total_ref[897:898, :]
    nbias_ref[...] = total_ref[898:899, :]
    ngain_ref[...] = total_ref[899:900, :]


def layer_kernel(
    scale,
    feat_ref, halo_ref, edge_ref, ncot_ref, ecot_ref, snd_ref, rcv_ref, cnt_ref,
    ein_ref, ebias_ref, eout_ref, egain_ref, nin_ref, nbias_ref, nout_ref, ngain_ref,
    own_ref, slot_ref, egrad_ref, wgrad_ref,
    table, both, edge_hl, hid_hl, dsilu_s, xhat_s, rstd_s, msg_hl, dout_hl, dpre_hl, up_s, recv_s,
):
    cells, halo = feat_ref.shape[0], halo_ref.shape[0]
    edges = edge_ref.shape[0]
    tbl = cells + halo
    sub = CHUNK // LANES
    eblocks = edges // LANES
    ein = ein_ref[...]
    w_e, w_s, w_r = ein[:LANES], ein[LANES : 2 * LANES], ein[2 * LANES :]
    eoc = centre(eout_ref[...])
    gain, bias = egain_ref[...], ebias_ref[...]

    table[:cells, :] = split(feat_ref[...])
    table[cells:, :] = split(halo_ref[...])
    both[:tbl, :] = split(halves(mul(table[...], dense(w_s))))
    both[tbl:, :] = split(halves(mul(table[:cells, :], dense(w_r))))
    we_cat, wo_cat = dense(w_e), dense(eoc)

    def valid_of(c):
        row = lax.broadcasted_iota(jnp.int32, (LANES, LANES), 0)
        return jnp.concatenate([jnp.where(row < cnt_ref[c * sub + k], 1.0, 0.0) for k in range(sub)], axis=0)

    def rcv_rows(c):
        return jnp.concatenate(
            [pick_rows(rcv_ref[pl.ds(c * sub + k, 1), :], cells // LANES) for k in range(sub)], axis=0
        )

    def forward(c, carry):
        at = pl.ds(pl.multiple_of(c * CHUNK, CHUNK), CHUNK)
        one = jnp.concatenate(
            [pick_rows(snd_ref[pl.ds(c * sub + k, 1), :], tbl // LANES) for k in range(sub)], axis=0
        )
        one = jnp.concatenate([one, rcv_rows(c)], axis=1)
        feat = split(edge_ref[at, :])
        edge_hl[at, :] = feat
        pre = halves(mul(one, both[...]) + mul(feat, we_cat)) + bias
        sig = jax.nn.sigmoid(pre)
        hid = pre * sig
        dsilu_s[at, :] = sig + hid * (1.0 - sig)
        hid = split(hid)
        hid_hl[at, :] = hid
        out = halves(mul(hid, wo_cat))
        rstd = lax.rsqrt(jnp.mean(out * out, axis=-1, keepdims=True) + NORM_EPS)
        xhat = out * rstd
        rstd_s[at, :] = jnp.broadcast_to(rstd, out.shape)
        xhat_s[at, :] = xhat
        msg_hl[at, :] = split(xhat * gain * valid_of(c))
        return carry

    lax.fori_loop(0, edges // CHUNK, forward, 0)

    summed = jnp.concatenate(
        [halves(mul(pick_cols(rcv_ref, t, eblocks), msg_hl[...])) for t in range(cells // LANES)], axis=0
    )
    nin, ngain = nin_ref[...], ngain_ref[...]
    noc = centre(nout_ref[...])
    feat_hl, sum_hl = table[:cells, :], split(summed)
    pre = halves(mul(feat_hl, dense(nin[:LANES])) + mul(sum_hl, dense(nin[LANES:]))) + nbias_ref[...]
    sig = jax.nn.sigmoid(pre)
    hid = pre * sig
    dsilu = sig + hid * (1.0 - sig)
    hid = split(hid)
    out = halves(mul(hid, dense(noc)))
    rstd = lax.rsqrt(jnp.mean(out * out, axis=-1, keepdims=True) + NORM_EPS)
    xhat = out * rstd
    ncot = ncot_ref[...]
    dn = ncot * ngain
    dout = split(rstd * (dn - xhat * jnp.mean(dn * xhat, axis=-1, keepdims=True)))
    dpre = halves(mul(dout, dense(noc.T))) * dsilu
    dpre_n = split(dpre)
    own_ref[...] = ncot + halves(mul(dpre_n, dense(nin[:LANES].T)))
    dsum = split(halves(mul(dpre_n, dense(nin[LANES:].T))))
    wgrad_ref[512:640, :] = mul_t(feat_hl, dpre_n) * scale
    wgrad_ref[640:768, :] = mul_t(sum_hl, dpre_n) * scale
    wgrad_ref[768:896, :] = centre(mul_t(hid, dout)) * scale
    nbias_g = jnp.sum(dpre, axis=0, keepdims=True)
    ngain_g = jnp.sum(ncot * xhat, axis=0, keepdims=True)

    wot_cat, wet_cat = dense(eoc.T), dense(w_e.T)

    def backward(c, carry):
        bias_g, gain_g = carry
        at = pl.ds(pl.multiple_of(c * CHUNK, CHUNK), CHUNK)
        ecot = ecot_ref[at, :]
        xhat = xhat_s[at, :]
        dm = (ecot + halves(mul(rcv_rows(c), dsum))) * valid_of(c)
        dn = dm * gain
        dout = split(rstd_s[at, :] * (dn - xhat * jnp.mean(dn * xhat, axis=-1, keepdims=True)))
        dout_hl[at, :] = dout
        dpre = halves(mul(dout, wot_cat)) * dsilu_s[at, :]
        dpre_c = split(dpre)
        dpre_hl[at, :] = dpre_c
        egrad_ref[at, :] = ecot + halves(mul(dpre_c, wet_cat))
        fold = lambda x: jnp.sum(x.reshape(CHUNK // 8, 8, LANES), axis=0)
        return bias_g + fold(dpre), gain_g + fold(dm * xhat)

    zero = jnp.zeros((8, LANES), F32)
    ebias_g, egain_g = lax.fori_loop(0, edges // CHUNK, backward, (zero, zero))

    wgrad_ref[384:512, :] = centre(mul_t(hid_hl[...], dout_hl[...])) * scale
    wgrad_ref[0:128, :] = mul_t(edge_hl[...], dpre_hl[...]) * scale
    wgrad_ref[904:, :] = jnp.zeros((wgrad_ref.shape[0] - 904, LANES), F32)
    wgrad_ref[896:904, :] = jnp.concatenate(
        [
            jnp.sum(ebias_g, axis=0, keepdims=True),
            jnp.sum(egain_g, axis=0, keepdims=True),
            nbias_g,
            ngain_g,
            jnp.zeros((4, LANES), F32),
        ],
        axis=0,
    ) * scale

    def up(t, carry):
        out = pl.ds(pl.multiple_of(t * LANES, LANES), LANES)
        up_s[out, :] = split(halves(mul(pick_cols(snd_ref, t, eblocks), dpre_hl[...])))
        return carry

    lax.fori_loop(0, tbl // LANES, up, 0)

    def down(t, carry):
        out = pl.ds(pl.multiple_of(t * LANES, LANES), LANES)
        recv_s[out, :] = split(halves(mul(pick_cols(rcv_ref, t, eblocks), dpre_hl[...])))
        return carry

    lax.fori_loop(0, cells // LANES, down, 0)

    wst = dense(w_s.T)
    own_ref[...] += halves(mul(up_s[:cells, :], wst) + mul(recv_s[...], dense(w_r.T)))
    slot_ref[...] = halves(mul(up_s[cells:, :], wst))
    wgrad_ref[128:256, :] = mul_t(table[...], up_s[...]) * scale
    wgrad_ref[256:384, :] = mul_t(table[:cells, :], recv_s[...]) * scale


def on_device(
    node_feat, edge_feat, node_cot, edge_cot, sender, receiver, block_count, send_rows,
    edge_in_weight, edge_bias, edge_out_weight, edge_gain,
    node_in_weight, node_bias, node_out_weight, node_gain,
):
    cells, width = node_feat.shape
    edges = edge_feat.shape[0]
    slots = send_rows.shape[3]
    total = lax.axis_size("gx") * lax.axis_size("gy") * lax.axis_size("gz") * edges
    scale = 1.0 / math.sqrt(total)
    halo = -(-27 * slots // LANES) * LANES
    rows = jnp.where((jnp.arange(27) != 13)[:, None], send_rows.reshape(27, slots), -1).reshape(27 * slots)
    rows = jnp.pad(rows, (0, halo - 27 * slots), constant_values=-1).reshape(halo // LANES, LANES)

    sizes = tuple(lax.axis_size(axis) for axis in AXES)
    link = [pltpu.VMEM((27, slots, width), F32)] * 2 + [pltpu.SemaphoreType.DMA((27,))] * 2
    received = pl.pallas_call(
        functools.partial(pack_kernel, sizes),
        out_shape=jax.ShapeDtypeStruct((halo, width), F32),
        in_specs=[VMEM] * 2,
        out_specs=VMEM,
        scratch_shapes=link,
        compiler_params=pltpu.CompilerParams(collective_id=0, has_side_effects=True),
        name="pack",
    )(node_feat, rows)
    tbl = cells + halo
    big = lambda dtype, cols: pltpu.VMEM((edges, cols), dtype)
    own, slot, edge_grad, wgrad = pl.pallas_call(
        functools.partial(layer_kernel, scale),
        out_shape=(
            jax.ShapeDtypeStruct((cells, width), F32),
            jax.ShapeDtypeStruct((halo, width), F32),
            jax.ShapeDtypeStruct((edges, width), F32),
            jax.ShapeDtypeStruct((GRAD_ROWS, width), F32),
        ),
        in_specs=[VMEM] * 7 + [pl.BlockSpec(memory_space=pltpu.SMEM)] + [VMEM] * 8,
        out_specs=(VMEM,) * 4,
        scratch_shapes=[
            pltpu.VMEM((tbl, 256), BF16),
            pltpu.VMEM((tbl + cells, 256), BF16),
            big(BF16, 256),
            big(BF16, 256),
            big(F32, 128),
            big(F32, 128),
            big(F32, 128),
            big(BF16, 256),
            big(BF16, 256),
            big(BF16, 256),
            pltpu.VMEM((tbl, 256), BF16),
            pltpu.VMEM((cells, 256), BF16),
        ],
        compiler_params=pltpu.CompilerParams(vmem_limit_bytes=48 * 1024 * 1024),
        name="layer",
    )(
        node_feat, received, edge_feat, node_cot, edge_cot,
        sender.reshape(edges // LANES, LANES), receiver.reshape(edges // LANES, LANES), block_count,
        edge_in_weight, edge_bias.reshape(1, width), edge_out_weight, edge_gain.reshape(1, width),
        node_in_weight, node_bias.reshape(1, width), node_out_weight, node_gain.reshape(1, width),
    )
    plan = sum_plan(sizes, GRAD_ROWS)
    total_grad, back = pl.pallas_call(
        functools.partial(sum_kernel, sizes, plan),
        out_shape=(jax.ShapeDtypeStruct((GRAD_ROWS, width), F32), jax.ShapeDtypeStruct((halo, width), F32)),
        in_specs=[VMEM] * 2,
        out_specs=(VMEM, VMEM),
        scratch_shapes=[
            pltpu.VMEM((GRAD_ROWS, width), F32),
            pltpu.VMEM((GRAD_ROWS, width), F32),
            pltpu.VMEM((plan[4], width), F32),
        ]
        + link
        + [pltpu.SemaphoreType.DMA((plan[5],))] * 2,
        compiler_params=pltpu.CompilerParams(collective_id=1, has_side_effects=True),
        name="sum",
    )(wgrad, slot)
    line = jax.ShapeDtypeStruct((1, width), F32)
    square = lambda r: jax.ShapeDtypeStruct((r, width), F32)
    node_grad, ein, ebias, eout, egain, nin, nbias, nout, ngain = pl.pallas_call(
        finish_kernel,
        out_shape=(square(cells), square(384), line, square(128), line, square(256), line, square(128), line),
        in_specs=[VMEM] * 4,
        out_specs=(VMEM,) * 9,
        name="finish",
    )(own, back, rows, total_grad)
    flat = lambda x: x.reshape(width)
    return (node_grad, edge_grad, ein, flat(ebias), eout, flat(egain), nin, flat(nbias), nout, flat(ngain))


def solution(mesh):
    part = P(AXES, None)
    flat = P(AXES)
    return jax.shard_map(
        on_device,
        mesh=mesh,
        in_specs=(part,) * 4 + (flat,) * 3 + (P("gx", "gy", "gz", None),) + (P(),) * 8,
        out_specs=(part,) * 2 + (P(),) * 8,
        check_vma=False,
    )
```

```python
import functools
import math

import jax
import jax.numpy as jnp
from jax import lax
from jax.experimental import pallas as pl
from jax.experimental.pallas import tpu as pltpu
from jax.sharding import PartitionSpec as P

NORM_EPS = 1e-05
LANES = 128
CHUNK = 512
AXES = ("gx", "gy", "gz")
F32, BF16 = jnp.float32, jnp.bfloat16
VMEM = pl.BlockSpec(memory_space=pltpu.VMEM)


def split(x):
    high = x.astype(BF16)
    low = (x - high.astype(F32)).astype(BF16)
    return jnp.concatenate([high, low], axis=1)


def dense(w):
    row = split(w)
    return jnp.concatenate([row, row], axis=0)


def halves(y):
    return y[:, :LANES] + y[:, LANES:]


def mul(a, b):
    return jnp.dot(a, b, preferred_element_type=F32)


def mul_t(a, b):
    y = lax.dot_general(a, b, (((0,), (0,)), ((), ())), preferred_element_type=F32)
    return halves(y[:LANES] + y[LANES:])


def hot(mask):
    return jnp.where(mask, 1.0, 0.0).astype(BF16)


def pick_rows(idx_row, blocks):
    col = jnp.broadcast_to(idx_row, (LANES, LANES)).T
    lane = lax.broadcasted_iota(jnp.int32, (LANES, LANES), 1)
    return jnp.concatenate([hot(col == lane + LANES * k) for k in range(blocks)], axis=1)


def pick_cols(idx_ref, tile, blocks):
    row = lax.broadcasted_iota(jnp.int32, (LANES, LANES), 0) + LANES * tile
    return jnp.concatenate(
        [hot(jnp.broadcast_to(idx_ref[b : b + 1, :], (LANES, LANES)) == row) for b in range(blocks)],
        axis=1,
    )


def centre(x):
    return x - jnp.mean(x, axis=-1, keepdims=True)


def position(sizes):
    return tuple(lax.axis_index(axis) for axis in AXES), sizes


def directions(spot):
    at, sizes = spot
    for d in range(27):
        if d == 13:
            continue
        step = (d // 9 - 1, d // 3 % 3 - 1, d % 3 - 1)
        if any(n == 1 and s != 0 for n, s in zip(sizes, step)):
            continue
        inside = None
        for p, n, s in zip(at, sizes, step):
            if s:
                ok = p > 0 if s < 0 else p < n - 1
                inside = ok if inside is None else jnp.logical_and(inside, ok)
        yield d, inside, tuple(p + s for p, s in zip(at, step))


def greet_neighbours(spot, barrier):
    for _, inside, where in directions(spot):

        @pl.when(inside)
        def _():
            pl.semaphore_signal(barrier, inc=1, device_id=where, device_id_type=pl.DeviceIdType.MESH)

    count = 1
    for p, n in zip(*spot):
        count = count * (1 + (p > 0).astype(jnp.int32) + (p < n - 1).astype(jnp.int32))
    return count - 1


def halo_copy(d, where, out, land, send, recv):
    return pltpu.make_async_remote_copy(
        src_ref=out.at[d], dst_ref=land.at[26 - d], send_sem=send.at[d], recv_sem=recv.at[26 - d],
        device_id=where, device_id_type=pl.DeviceIdType.MESH,
    )


def halo_start(spot, out, land, send, recv):
    for d, inside, where in directions(spot):

        @pl.when(inside)
        def _():
            halo_copy(d, where, out, land, send, recv).start()


def halo_wait(spot, out, land, send, recv):
    for d, inside, where in directions(spot):

        @pl.when(inside)
        def _():
            halo_copy(d, where, out, land, send, recv).wait_send()
            halo_copy(26 - d, where, out, land, send, recv).wait_recv()


def sum_plan(sizes, rows, slot, sem):
    bits = []
    for axis in (1, 0, 2):
        stride = 1
        while stride < sizes[axis]:
            bits.append((axis, stride))
            stride *= 2
    groups = [bits[:1]] + [bits[i : i + 2] for i in range(1, len(bits), 2)]
    steps, r = [], rows
    for group in groups:
        n = 2 ** len(group)
        scatters = r > 64 and r % (8 * n) == 0
        r = r // n if scatters else r
        steps.append((tuple(group), scatters, r, slot, sem))
        slot, sem = slot + (n - 1) * r, sem + 2 * (n - 1)
    return steps, slot, sem


def peers_of(at, group):
    own = [lax.rem(at[axis] // stride, 2) for axis, stride in group]
    digit = sum(b * 2**i for i, b in enumerate(own))
    others = []
    for k in range(1, 2 ** len(group)):
        where, other = list(at), 0
        for i, (axis, stride) in enumerate(group):
            bit = own[i]
            if k >> i & 1:
                where[axis] = where[axis] + (1 - 2 * bit) * stride
                bit = 1 - bit
            other = other + bit * 2**i
        others.append((k, other, tuple(where)))
    return digit, others


def summing(at, steps, acc, full, rbuf, sems, rsems):
    def block(ref, start, r):
        return ref.at[pl.ds(pl.multiple_of(start, 8), r)]

    def remote(src, dst, sem, where):
        return pltpu.make_async_remote_copy(
            src_ref=src, dst_ref=dst, send_sem=sems.at[sem], recv_sem=rsems.at[sem],
            device_id=where, device_id_type=pl.DeviceIdType.MESH,
        )

    off = 0
    for group, scatters, r, slot, sem in steps:
        digit, others = peers_of(at, group)
        copies = [
            remote(
                block(acc, off + other * r if scatters else off, r),
                rbuf.at[pl.ds(slot + (k - 1) * r, r)], sem + k - 1, where,
            )
            for k, other, where in others
        ]
        for copy in copies:
            copy.start()
        yield
        for copy in copies:
            copy.wait()
        off = off + digit * r if scatters else off
        here = pl.ds(pl.multiple_of(off, 8), r)
        terms = [acc[here, :]] + [rbuf[slot + k * r : slot + (k + 1) * r, :] for k in range(len(others))]
        while len(terms) > 1:
            terms = [terms[i] + terms[i + 1] for i in range(0, len(terms), 2)]
        acc[here, :] = terms[0]
    last = steps[-1][2]
    here = pl.ds(pl.multiple_of(off, 8), last)
    full[here, :] = acc[here, :]
    for group, scatters, r, slot, sem in reversed(steps):
        if not scatters:
            continue
        digit, others = peers_of(at, group)
        base = off - digit * r
        first = sem + len(others) - 1
        for k, other, where in others:
            remote(block(full, off, r), block(full, off, r), first + k, where).start()
        yield
        for k, other, where in others:
            remote(block(full, off, r), block(full, off, r), first + k, where).wait_send()
            came = block(full, base + other * r, r)
            remote(came, came, first + k, where).wait_recv()
        off = base


def advance(*sums):
    for one in sums:
        next(one, None)


def fused_kernel(
    sizes, plans, scale,
    feat_ref, edge_ref, ncot_ref, ecot_ref, snd_ref, rcv_ref, cnt_ref, rows_ref,
    ein_ref, ebias_ref, eout_ref, egain_ref, nin_ref, nbias_ref, nout_ref, ngain_ref,
    own_ref, egrad_ref, tot_e_ref, tot_n_ref, tot_v_ref,
    table, both, edge_f, ncot_f, ecot_f, egrad_f, edge_hl, hid_hl, dsilu_s, xhat_s, rstd_s,
    msg_hl, dout_hl, dpre_hl, up_s, recv_s,
    acc_e, acc_n, acc_v, full_e, full_n, full_v, rbuf,
    packets, land, slot_out, slot_in,
    load, store, send, recv, send2, recv2, sems, rsems,
):
    spot = position(sizes)
    at = spot[0]
    cells, edges = feat_ref.shape[0], edge_ref.shape[0]
    slots = packets.shape[1]
    halo = rows_ref.shape[0] * LANES
    tbl = cells + halo
    sub = CHUNK // LANES
    eblocks, cblocks = edges // LANES, cells // LANES
    chunks = edges // CHUNK

    loads = [
        pltpu.make_async_copy(src, dst, load.at[i])
        for i, (src, dst) in enumerate(((edge_ref, edge_f), (ncot_ref, ncot_f), (ecot_ref, ecot_f)))
    ]
    for copy in loads:
        copy.start()
    land[...] = jnp.zeros_like(land)
    slot_in[...] = jnp.zeros_like(slot_in)
    barrier = pltpu.get_barrier_semaphore()
    count = greet_neighbours(spot, barrier)
    for step in plans[0]:
        for _, _, where in peers_of(at, step[0])[1]:
            pl.semaphore_signal(barrier, inc=1, device_id=where, device_id_type=pl.DeviceIdType.MESH)
            count = count + 1

    table[:cells, :] = split(feat_ref[...])
    per = LANES // slots
    for b in range(rows_ref.shape[0]):
        picked = halves(mul(pick_rows(rows_ref[b : b + 1, :], cblocks), table[:cells, :]))
        for k in range(per):
            if b * per + k < 27:
                packets[b * per + k] = picked[k * slots : (k + 1) * slots]
    pl.semaphore_wait(barrier, count)
    halo_start(spot, packets, land, send, recv)

    ein = ein_ref[...]
    w_e, w_s, w_r = ein[:LANES], ein[LANES : 2 * LANES], ein[2 * LANES :]
    eoc = centre(eout_ref[...])
    gain, bias = egain_ref[...], ebias_ref[...]
    ws_cat, we_cat, wo_cat = dense(w_s), dense(w_e), dense(eoc)
    both[:cells, :] = split(halves(mul(table[:cells, :], ws_cat)))
    both[cells : 2 * cells, :] = split(halves(mul(table[:cells, :], dense(w_r))))
    loads[0].wait()

    def valid_of(c):
        row = lax.broadcasted_iota(jnp.int32, (LANES, LANES), 0)
        return jnp.concatenate([jnp.where(row < cnt_ref[c * sub + k], 1.0, 0.0) for k in range(sub)], axis=0)

    def picks(ref, c, low, blocks):
        return jnp.concatenate(
            [pick_rows(ref[pl.ds(c * sub + k, 1), :] - low, blocks) for k in range(sub)], axis=0
        )

    def before(c, carry):
        here = pl.ds(pl.multiple_of(c * CHUNK, CHUNK), CHUNK)
        one = jnp.concatenate([picks(snd_ref, c, 0, cblocks), picks(rcv_ref, c, 0, cblocks)], axis=1)
        feat = split(edge_f[here, :])
        edge_hl[here, :] = feat
        dsilu_s[here, :] = halves(mul(one, both[: 2 * cells, :]) + mul(feat, we_cat)) + bias
        return carry

    lax.fori_loop(0, chunks, before, 0)

    halo_wait(spot, packets, land, send, recv)
    table[cells : cells + 27 * slots, :] = split(land[...].reshape(27 * slots, LANES))
    table[cells + 27 * slots :, :] = jnp.zeros((halo - 27 * slots, 2 * LANES), BF16)
    both[2 * cells :, :] = split(halves(mul(table[cells:, :], ws_cat)))

    def forward(c, carry):
        here = pl.ds(pl.multiple_of(c * CHUNK, CHUNK), CHUNK)
        one = picks(snd_ref, c, cells, halo // LANES)
        pre = dsilu_s[here, :] + halves(mul(one, both[2 * cells :, :]))
        sig = jax.nn.sigmoid(pre)
        hid = pre * sig
        dsilu_s[here, :] = sig + hid * (1.0 - sig)
        hid = split(hid)
        hid_hl[here, :] = hid
        out = halves(mul(hid, wo_cat))
        rstd = lax.rsqrt(jnp.mean(out * out, axis=-1, keepdims=True) + NORM_EPS)
        xhat = out * rstd
        rstd_s[here, :] = jnp.broadcast_to(rstd, out.shape)
        xhat_s[here, :] = xhat
        msg_hl[here, :] = split(xhat * gain * valid_of(c))
        return carry

    lax.fori_loop(0, chunks, forward, 0)

    summed = jnp.concatenate(
        [halves(mul(pick_cols(rcv_ref, t, eblocks), msg_hl[...])) for t in range(cblocks)], axis=0
    )
    nin, ngain = nin_ref[...], ngain_ref[...]
    noc = centre(nout_ref[...])
    feat_hl, sum_hl = table[:cells, :], split(summed)
    pre = halves(mul(feat_hl, dense(nin[:LANES])) + mul(sum_hl, dense(nin[LANES:]))) + nbias_ref[...]
    sig = jax.nn.sigmoid(pre)
    hid = pre * sig
    dsilu = sig + hid * (1.0 - sig)
    hid = split(hid)
    out = halves(mul(hid, dense(noc)))
    rstd = lax.rsqrt(jnp.mean(out * out, axis=-1, keepdims=True) + NORM_EPS)
    xhat = out * rstd
    loads[1].wait()
    ncot = ncot_f[...]
    dn = ncot * ngain
    dout = split(rstd * (dn - xhat * jnp.mean(dn * xhat, axis=-1, keepdims=True)))
    dpre = halves(mul(dout, dense(noc.T))) * dsilu
    dpre_n = split(dpre)
    dsum = split(halves(mul(dpre_n, dense(nin[LANES:].T))))
    acc_n[0:128, :] = mul_t(feat_hl, dpre_n) * scale
    acc_n[128:256, :] = mul_t(sum_hl, dpre_n) * scale
    acc_n[256:384, :] = centre(mul_t(hid, dout)) * scale
    node_sum = summing(at, plans[1], acc_n, full_n, rbuf, sems, rsems)
    advance(node_sum)
    own_ref[...] = ncot + halves(mul(dpre_n, dense(nin[:LANES].T)))
    nbias_g = jnp.sum(dpre, axis=0, keepdims=True)
    ngain_g = jnp.sum(ncot * xhat, axis=0, keepdims=True)

    wot_cat, wet_cat = dense(eoc.T), dense(w_e.T)
    loads[2].wait()

    def backward(c, carry):
        bias_g, gain_g = carry
        here = pl.ds(pl.multiple_of(c * CHUNK, CHUNK), CHUNK)
        ecot = ecot_f[here, :]
        xhat = xhat_s[here, :]
        dm = (ecot + halves(mul(picks(rcv_ref, c, 0, cblocks), dsum))) * valid_of(c)
        dn = dm * gain
        dout = split(rstd_s[here, :] * (dn - xhat * jnp.mean(dn * xhat, axis=-1, keepdims=True)))
        dout_hl[here, :] = dout
        dpre = halves(mul(dout, wot_cat)) * dsilu_s[here, :]
        dpre_c = split(dpre)
        dpre_hl[here, :] = dpre_c
        egrad_f[here, :] = ecot + halves(mul(dpre_c, wet_cat))
        fold = lambda x: jnp.sum(x.reshape(CHUNK // 8, 8, LANES), axis=0)
        return bias_g + fold(dpre), gain_g + fold(dm * xhat)

    zero = jnp.zeros((8, LANES), F32)
    sums = lax.fori_loop(0, chunks // 2, backward, (zero, zero))
    advance(node_sum)
    ebias_g, egain_g = lax.fori_loop(chunks // 2, chunks, backward, sums)
    advance(node_sum)
    out_copy = pltpu.make_async_copy(egrad_f, egrad_ref, store.at[0])
    out_copy.start()

    def up(t, carry):
        out = pl.ds(pl.multiple_of(t * LANES, LANES), LANES)
        up_s[out, :] = split(halves(mul(pick_cols(snd_ref, t, eblocks), dpre_hl[...])))
        return carry

    def down(t, carry):
        out = pl.ds(pl.multiple_of(t * LANES, LANES), LANES)
        recv_s[out, :] = split(halves(mul(pick_cols(rcv_ref, t, eblocks), dpre_hl[...])))
        return carry

    wst = dense(w_s.T)
    lax.fori_loop(cblocks, tbl // LANES, up, 0)
    slot_out[...] = halves(mul(up_s[cells : cells + 27 * slots, :], wst)).reshape(27, slots, LANES)
    halo_start(spot, slot_out, slot_in, send2, recv2)
    advance(node_sum)
    lax.fori_loop(0, cblocks, up, 0)
    lax.fori_loop(0, cblocks, down, 0)
    advance(node_sum)
    acc_e[0:128, :] = mul_t(edge_hl[...], dpre_hl[...]) * scale
    acc_e[128:256, :] = mul_t(table[...], up_s[...]) * scale
    acc_e[256:384, :] = mul_t(table[:cells, :], recv_s[...]) * scale
    acc_e[384:512, :] = centre(mul_t(hid_hl[...], dout_hl[...])) * scale
    acc_v[...] = jnp.concatenate(
        [
            jnp.sum(ebias_g, axis=0, keepdims=True),
            jnp.sum(egain_g, axis=0, keepdims=True),
            nbias_g,
            ngain_g,
            jnp.zeros((4, LANES), F32),
        ],
        axis=0,
    ) * scale
    edge_sum = summing(at, plans[0], acc_e, full_e, rbuf, sems, rsems)
    vec_sum = summing(at, plans[2], acc_v, full_v, rbuf, sems, rsems)
    advance(edge_sum, vec_sum)
    for _ in range(2 * len(plans[1])):
        advance(node_sum)
    own_ref[...] += halves(mul(up_s[:cells, :], wst) + mul(recv_s[...], dense(w_r.T)))
    advance(edge_sum, vec_sum)
    halo_wait(spot, slot_out, slot_in, send2, recv2)
    back = jnp.concatenate(
        [split(slot_in[...].reshape(27 * slots, LANES)), jnp.zeros((halo - 27 * slots, 2 * LANES), BF16)], axis=0
    )
    for t in range(cblocks):
        own_ref[t * LANES : (t + 1) * LANES, :] += halves(mul(pick_cols(rows_ref, t, halo // LANES), back))
    for _ in range(2 * len(plans[0])):
        advance(edge_sum, vec_sum)
    tot_e_ref[...] = full_e[...]
    tot_n_ref[...] = full_n[...]
    tot_v_ref[...] = full_v[...]
    out_copy.wait()


def finish_kernel(
    own_ref, edge_ref, node_ref, vec_ref,
    out_ref, ein_ref, ebias_ref, eout_ref, egain_ref, nin_ref, nbias_ref, nout_ref, ngain_ref,
):
    out_ref[...] = own_ref[...]
    ein_ref[...] = edge_ref[0:384, :]
    eout_ref[...] = edge_ref[384:512, :]
    nin_ref[...] = node_ref[0:256, :]
    nout_ref[...] = node_ref[256:384, :]
    for i, ref in enumerate((ebias_ref, egain_ref, nbias_ref, ngain_ref)):
        ref[...] = vec_ref[i : i + 1, :]


def on_device(
    node_feat, edge_feat, node_cot, edge_cot, sender, receiver, block_count, send_rows,
    edge_in_weight, edge_bias, edge_out_weight, edge_gain,
    node_in_weight, node_bias, node_out_weight, node_gain,
):
    cells, width = node_feat.shape
    edges = edge_feat.shape[0]
    slots = send_rows.shape[3]
    total = lax.axis_size("gx") * lax.axis_size("gy") * lax.axis_size("gz") * edges
    scale = 1.0 / math.sqrt(total)
    halo = -(-27 * slots // LANES) * LANES
    rows = jnp.where((jnp.arange(27) != 13)[:, None], send_rows.reshape(27, slots), -1).reshape(27 * slots)
    rows = jnp.pad(rows, (0, halo - 27 * slots), constant_values=-1).reshape(halo // LANES, LANES)

    sizes = tuple(lax.axis_size(axis) for axis in AXES)
    tbl = cells + halo
    plan_e, slot, sem = sum_plan(sizes, 512, 0, 0)
    plan_n, slot, sem = sum_plan(sizes, 384, slot, sem)
    plan_v, slot, sem = sum_plan(sizes, 8, slot, sem)
    link = [pltpu.VMEM((27, slots, width), F32)] * 4
    dma = lambda n: pltpu.SemaphoreType.DMA((n,))
    big = lambda dtype, cols: pltpu.VMEM((edges, cols), dtype)
    keep = lambda r: pltpu.VMEM((r, width), F32)
    pair = lambda r: pltpu.VMEM((r, 2 * width), BF16)
    hbm = pl.BlockSpec(memory_space=pl.ANY)
    square = lambda r: jax.ShapeDtypeStruct((r, width), F32)
    own, edge_grad, tot_e, tot_n, tot_v = pl.pallas_call(
        functools.partial(fused_kernel, sizes, (plan_e, plan_n, plan_v), scale),
        out_shape=(square(cells), square(edges), square(512), square(384), square(8)),
        in_specs=[VMEM, hbm, hbm, hbm, VMEM, VMEM, pl.BlockSpec(memory_space=pltpu.SMEM), VMEM] + [VMEM] * 8,
        out_specs=(VMEM, hbm, VMEM, VMEM, VMEM),
        scratch_shapes=[
            pair(tbl), pair(tbl + cells), keep(edges), keep(cells), keep(edges), keep(edges),
            pair(edges), pair(edges), keep(edges), keep(edges), keep(edges),
            pair(edges), pair(edges), pair(edges), pair(tbl), pair(cells),
            keep(512), keep(384), keep(8), keep(512), keep(384), keep(8), keep(slot),
        ]
        + link
        + [dma(3), dma(1), dma(27), dma(27), dma(27), dma(27), dma(sem), dma(sem)],
        compiler_params=pltpu.CompilerParams(
            collective_id=0, has_side_effects=True, vmem_limit_bytes=56 * 1024 * 1024
        ),
        name="layer",
    )(
        node_feat, edge_feat, node_cot, edge_cot,
        sender.reshape(edges // LANES, LANES), receiver.reshape(edges // LANES, LANES), block_count, rows,
        edge_in_weight, edge_bias.reshape(1, width), edge_out_weight, edge_gain.reshape(1, width),
        node_in_weight, node_bias.reshape(1, width), node_out_weight, node_gain.reshape(1, width),
    )
    line = jax.ShapeDtypeStruct((1, width), F32)
    node_grad, ein, ebias, eout, egain, nin, nbias, nout, ngain = pl.pallas_call(
        finish_kernel,
        out_shape=(square(cells), square(384), line, square(128), line, square(256), line, square(128), line),
        in_specs=[VMEM] * 4,
        out_specs=(VMEM,) * 9,
        name="finish",
    )(own, tot_e, tot_n, tot_v)
    flat = lambda x: x.reshape(width)
    return (node_grad, edge_grad, ein, flat(ebias), eout, flat(egain), nin, flat(nbias), nout, flat(ngain))


def solution(mesh):
    part = P(AXES, None)
    flat = P(AXES)
    return jax.shard_map(
        on_device,
        mesh=mesh,
        in_specs=(part,) * 4 + (flat,) * 3 + (P("gx", "gy", "gz", None),) + (P(),) * 8,
        out_specs=(part,) * 2 + (P(),) * 8,
        check_vma=False,
    )
```

```python
import functools
import math

import jax
import jax.numpy as jnp
from jax import lax
from jax.experimental import pallas as pl
from jax.experimental.pallas import tpu as pltpu
from jax.sharding import PartitionSpec as P

NORM_EPS = 1e-05
LANES = 128
CHUNK = 512
AXES = ("gx", "gy", "gz")
F32, BF16 = jnp.float32, jnp.bfloat16
VMEM = pl.BlockSpec(memory_space=pltpu.VMEM)


def split(x):
    high = x.astype(BF16)
    low = (x - high.astype(F32)).astype(BF16)
    return jnp.concatenate([high, low], axis=1)


def dense(w):
    row = split(w)
    return jnp.concatenate([row, row], axis=0)


def halves(y):
    return y[:, :LANES] + y[:, LANES:]


def mul(a, b):
    return jnp.dot(a, b, preferred_element_type=F32)


def mul_t(a, b):
    y = lax.dot_general(a, b, (((0,), (0,)), ((), ())), preferred_element_type=F32)
    return halves(y[:LANES] + y[LANES:])


def hot(mask):
    return jnp.where(mask, 1.0, 0.0).astype(BF16)


def pick_rows(idx_row, blocks):
    col = jnp.broadcast_to(idx_row, (LANES, LANES)).T
    lane = lax.broadcasted_iota(jnp.int32, (LANES, LANES), 1)
    return jnp.concatenate([hot(col == lane + LANES * k) for k in range(blocks)], axis=1)


def pick_cols(idx_ref, tile, blocks):
    row = lax.broadcasted_iota(jnp.int32, (LANES, LANES), 0) + LANES * tile
    return jnp.concatenate(
        [hot(jnp.broadcast_to(idx_ref[b : b + 1, :], (LANES, LANES)) == row) for b in range(blocks)],
        axis=1,
    )


def centre(x):
    return x - jnp.mean(x, axis=-1, keepdims=True)


def position(sizes):
    return tuple(lax.axis_index(axis) for axis in AXES), sizes


def directions(spot):
    at, sizes = spot
    for d in range(27):
        if d == 13:
            continue
        step = (d // 9 - 1, d // 3 % 3 - 1, d % 3 - 1)
        if any(n == 1 and s != 0 for n, s in zip(sizes, step)):
            continue
        inside = None
        for p, n, s in zip(at, sizes, step):
            if s:
                ok = p > 0 if s < 0 else p < n - 1
                inside = ok if inside is None else jnp.logical_and(inside, ok)
        yield d, inside, tuple(p + s for p, s in zip(at, step))


def greet_neighbours(spot, barrier):
    for _, inside, where in directions(spot):

        @pl.when(inside)
        def _():
            pl.semaphore_signal(barrier, inc=1, device_id=where, device_id_type=pl.DeviceIdType.MESH)

    count = 1
    for p, n in zip(*spot):
        count = count * (1 + (p > 0).astype(jnp.int32) + (p < n - 1).astype(jnp.int32))
    return count - 1


def halo_copy(d, where, out, land, send, recv):
    return pltpu.make_async_remote_copy(
        src_ref=out.at[d], dst_ref=land.at[26 - d], send_sem=send.at[d], recv_sem=recv.at[26 - d],
        device_id=where, device_id_type=pl.DeviceIdType.MESH,
    )


def halo_start(spot, out, land, send, recv):
    for d, inside, where in directions(spot):

        @pl.when(inside)
        def _():
            halo_copy(d, where, out, land, send, recv).start()


def halo_wait(spot, out, land, send, recv):
    for d, inside, where in directions(spot):

        @pl.when(inside)
        def _():
            halo_copy(d, where, out, land, send, recv).wait_send()
            halo_copy(26 - d, where, out, land, send, recv).wait_recv()


def sum_plan(sizes, rows, slot, sem):
    bits = []
    for axis in (1, 0, 2):
        stride = 1
        while stride < sizes[axis]:
            bits.append((axis, stride))
            stride *= 2
    groups = [bits[i : i + 3] for i in range(0, len(bits), 3)]
    steps, r = [], rows
    for group in groups:
        n = 2 ** len(group)
        scatters = r > 64 and r % (8 * n) == 0
        r = r // n if scatters else r
        steps.append((tuple(group), scatters, r, slot, sem))
        slot, sem = slot + (n - 1) * r, sem + 2 * (n - 1)
    return steps, slot, sem


def peers_of(at, group):
    own = [lax.rem(at[axis] // stride, 2) for axis, stride in group]
    digit = sum(b * 2**i for i, b in enumerate(own))
    others = []
    for k in range(1, 2 ** len(group)):
        where, other = list(at), 0
        for i, (axis, stride) in enumerate(group):
            bit = own[i]
            if k >> i & 1:
                where[axis] = where[axis] + (1 - 2 * bit) * stride
                bit = 1 - bit
            other = other + bit * 2**i
        others.append((k, other, tuple(where)))
    return digit, others


def summing(at, steps, acc, full, rbuf, sems, rsems):
    def block(ref, start, r):
        return ref.at[pl.ds(pl.multiple_of(start, 8), r)]

    def remote(src, dst, sem, where):
        return pltpu.make_async_remote_copy(
            src_ref=src, dst_ref=dst, send_sem=sems.at[sem], recv_sem=rsems.at[sem],
            device_id=where, device_id_type=pl.DeviceIdType.MESH,
        )

    off = 0
    for group, scatters, r, slot, sem in steps:
        digit, others = peers_of(at, group)
        copies = [
            remote(
                block(acc, off + other * r if scatters else off, r),
                rbuf.at[pl.ds(slot + (k - 1) * r, r)], sem + k - 1, where,
            )
            for k, other, where in others
        ]
        for copy in copies:
            copy.start()
        yield
        for copy in copies:
            copy.wait()
        off = off + digit * r if scatters else off
        here = pl.ds(pl.multiple_of(off, 8), r)
        terms = [acc[here, :]] + [rbuf[slot + k * r : slot + (k + 1) * r, :] for k in range(len(others))]
        while len(terms) > 1:
            terms = [terms[i] + terms[i + 1] for i in range(0, len(terms), 2)]
        acc[here, :] = terms[0]
    last = steps[-1][2]
    here = pl.ds(pl.multiple_of(off, 8), last)
    full[here, :] = acc[here, :]
    for group, scatters, r, slot, sem in reversed(steps):
        if not scatters:
            continue
        digit, others = peers_of(at, group)
        base = off - digit * r
        first = sem + len(others) - 1
        for k, other, where in others:
            remote(block(full, off, r), block(full, off, r), first + k, where).start()
        yield
        for k, other, where in others:
            remote(block(full, off, r), block(full, off, r), first + k, where).wait_send()
            came = block(full, base + other * r, r)
            remote(came, came, first + k, where).wait_recv()
        off = base


def advance(*sums):
    for one in sums:
        next(one, None)


def fused_kernel(
    sizes, plans, scale,
    feat_ref, edge_ref, ncot_ref, ecot_ref, snd_ref, rcv_ref, cnt_ref, rows_ref,
    ein_ref, ebias_ref, eout_ref, egain_ref, nin_ref, nbias_ref, nout_ref, ngain_ref,
    own_ref, egrad_ref, tot_e_ref, tot_o_ref, tot_n_ref, tot_m_ref,
    tot_ebias_ref, tot_egain_ref, tot_nbias_ref, tot_ngain_ref,
    table, both, edge_f, ncot_f, ecot_f, egrad_f, edge_hl, hid_hl, dsilu_s, xhat_s, rstd_s,
    msg_hl, dout_hl, dpre_hl, up_s, recv_s,
    acc_e, acc_t, acc_n, acc_v, full_e, full_t, full_n, full_v, rbuf,
    packets, land, slot_out, slot_in,
    load, store, send, recv, send2, recv2, sems, rsems,
):
    spot = position(sizes)
    at = spot[0]
    cells, edges = feat_ref.shape[0], edge_ref.shape[0]
    slots = packets.shape[1]
    halo = rows_ref.shape[0] * LANES
    tbl = cells + halo
    sub = CHUNK // LANES
    eblocks, cblocks = edges // LANES, cells // LANES
    chunks = edges // CHUNK

    loads = [
        pltpu.make_async_copy(src, dst, load.at[i])
        for i, (src, dst) in enumerate(((edge_ref, edge_f), (ncot_ref, ncot_f), (ecot_ref, ecot_f)))
    ]
    for copy in loads:
        copy.start()
    land[...] = jnp.zeros_like(land)
    slot_in[...] = jnp.zeros_like(slot_in)
    barrier = pltpu.get_barrier_semaphore()
    count = greet_neighbours(spot, barrier)
    for step in plans[0]:
        for _, _, where in peers_of(at, step[0])[1]:
            pl.semaphore_signal(barrier, inc=1, device_id=where, device_id_type=pl.DeviceIdType.MESH)
            count = count + 1

    table[:cells, :] = split(feat_ref[...])
    per = LANES // slots
    for b in range(rows_ref.shape[0]):
        picked = halves(mul(pick_rows(rows_ref[b : b + 1, :], cblocks), table[:cells, :]))
        for k in range(per):
            if b * per + k < 27:
                packets[b * per + k] = picked[k * slots : (k + 1) * slots]
    pl.semaphore_wait(barrier, count)
    halo_start(spot, packets, land, send, recv)

    ein = ein_ref[...]
    w_e, w_s, w_r = ein[:LANES], ein[LANES : 2 * LANES], ein[2 * LANES :]
    eoc = centre(eout_ref[...])
    gain, bias = egain_ref[...], ebias_ref[...]
    ws_cat, we_cat, wo_cat = dense(w_s), dense(w_e), dense(eoc)
    both[:cells, :] = split(halves(mul(table[:cells, :], ws_cat)))
    both[cells : 2 * cells, :] = split(halves(mul(table[:cells, :], dense(w_r))))
    loads[0].wait()

    def valid_of(c):
        row = lax.broadcasted_iota(jnp.int32, (LANES, LANES), 0)
        return jnp.concatenate([jnp.where(row < cnt_ref[c * sub + k], 1.0, 0.0) for k in range(sub)], axis=0)

    def picks(ref, c, low, blocks):
        return jnp.concatenate(
            [pick_rows(ref[pl.ds(c * sub + k, 1), :] - low, blocks) for k in range(sub)], axis=0
        )

    def before(c, carry):
        here = pl.ds(pl.multiple_of(c * CHUNK, CHUNK), CHUNK)
        one = jnp.concatenate([picks(snd_ref, c, 0, cblocks), picks(rcv_ref, c, 0, cblocks)], axis=1)
        feat = split(edge_f[here, :])
        edge_hl[here, :] = feat
        dsilu_s[here, :] = halves(mul(one, both[: 2 * cells, :]) + mul(feat, we_cat)) + bias
        return carry

    lax.fori_loop(0, chunks, before, 0)

    halo_wait(spot, packets, land, send, recv)
    table[cells : cells + 27 * slots, :] = split(land[...].reshape(27 * slots, LANES))
    table[cells + 27 * slots :, :] = jnp.zeros((halo - 27 * slots, 2 * LANES), BF16)
    both[2 * cells :, :] = split(halves(mul(table[cells:, :], ws_cat)))

    def forward(c, carry):
        here = pl.ds(pl.multiple_of(c * CHUNK, CHUNK), CHUNK)
        one = picks(snd_ref, c, cells, halo // LANES)
        pre = dsilu_s[here, :] + halves(mul(one, both[2 * cells :, :]))
        sig = jax.nn.sigmoid(pre)
        hid = pre * sig
        dsilu_s[here, :] = sig + hid * (1.0 - sig)
        hid = split(hid)
        hid_hl[here, :] = hid
        out = halves(mul(hid, wo_cat))
        rstd = lax.rsqrt(jnp.mean(out * out, axis=-1, keepdims=True) + NORM_EPS)
        xhat = out * rstd
        rstd_s[here, :] = jnp.broadcast_to(rstd, out.shape)
        xhat_s[here, :] = xhat
        msg_hl[here, :] = split(xhat * gain * valid_of(c))
        return carry

    lax.fori_loop(0, chunks, forward, 0)

    def tall(ref, low, high):
        return jnp.concatenate([pick_cols(ref, t, eblocks) for t in range(low, high)], axis=0)

    summed = halves(mul(tall(rcv_ref, 0, cblocks), msg_hl[...]))
    nin, ngain = nin_ref[...], ngain_ref[...]
    noc = centre(nout_ref[...])
    feat_hl, sum_hl = table[:cells, :], split(summed)
    pre = halves(mul(feat_hl, dense(nin[:LANES])) + mul(sum_hl, dense(nin[LANES:]))) + nbias_ref[...]
    sig = jax.nn.sigmoid(pre)
    hid = pre * sig
    dsilu = sig + hid * (1.0 - sig)
    hid = split(hid)
    out = halves(mul(hid, dense(noc)))
    rstd = lax.rsqrt(jnp.mean(out * out, axis=-1, keepdims=True) + NORM_EPS)
    xhat = out * rstd
    loads[1].wait()
    ncot = ncot_f[...]
    dn = ncot * ngain
    dout = split(rstd * (dn - xhat * jnp.mean(dn * xhat, axis=-1, keepdims=True)))
    dpre = halves(mul(dout, dense(noc.T))) * dsilu
    dpre_n = split(dpre)
    dsum = split(halves(mul(dpre_n, dense(nin[LANES:].T))))
    acc_n[0:128, :] = mul_t(feat_hl, dpre_n) * scale
    acc_n[128:256, :] = mul_t(sum_hl, dpre_n) * scale
    acc_n[256:384, :] = centre(mul_t(hid, dout)) * scale
    node_sum = summing(at, plans[2], acc_n, full_n, rbuf, sems, rsems)
    advance(node_sum)
    own_ref[...] = ncot + halves(mul(dpre_n, dense(nin[:LANES].T)))
    nbias_g = jnp.sum(dpre, axis=0, keepdims=True)
    ngain_g = jnp.sum(ncot * xhat, axis=0, keepdims=True)

    wot_cat, wet_cat = dense(eoc.T), dense(w_e.T)
    loads[2].wait()

    def backward(c, carry):
        bias_g, gain_g = carry
        here = pl.ds(pl.multiple_of(c * CHUNK, CHUNK), CHUNK)
        ecot = ecot_f[here, :]
        xhat = xhat_s[here, :]
        dm = (ecot + halves(mul(picks(rcv_ref, c, 0, cblocks), dsum))) * valid_of(c)
        dn = dm * gain
        dout = split(rstd_s[here, :] * (dn - xhat * jnp.mean(dn * xhat, axis=-1, keepdims=True)))
        dout_hl[here, :] = dout
        dpre = halves(mul(dout, wot_cat)) * dsilu_s[here, :]
        dpre_c = split(dpre)
        dpre_hl[here, :] = dpre_c
        egrad_f[here, :] = ecot + halves(mul(dpre_c, wet_cat))
        fold = lambda x: jnp.sum(x.reshape(CHUNK // 8, 8, LANES), axis=0)
        return bias_g + fold(dpre), gain_g + fold(dm * xhat)

    zero = jnp.zeros((8, LANES), F32)
    sums = lax.fori_loop(0, chunks // 2, backward, (zero, zero))
    advance(node_sum)
    ebias_g, egain_g = lax.fori_loop(chunks // 2, chunks, backward, sums)
    advance(node_sum)
    out_copy = pltpu.make_async_copy(egrad_f, egrad_ref, store.at[0])
    out_copy.start()

    wst = dense(w_s.T)
    up_s[cells:, :] = split(halves(mul(tall(snd_ref, cblocks, tbl // LANES), dpre_hl[...])))
    slot_out[...] = halves(mul(up_s[cells : cells + 27 * slots, :], wst)).reshape(27, slots, LANES)
    halo_start(spot, slot_out, slot_in, send2, recv2)
    advance(node_sum)
    acc_e[0:128, :] = mul_t(edge_hl[...], dpre_hl[...]) * scale
    acc_e[128:256, :] = centre(mul_t(hid_hl[...], dout_hl[...])) * scale
    acc_v[...] = jnp.concatenate(
        [
            jnp.sum(ebias_g, axis=0, keepdims=True),
            jnp.sum(egain_g, axis=0, keepdims=True),
            nbias_g,
            ngain_g,
            jnp.zeros((4, LANES), F32),
        ],
        axis=0,
    ) * scale
    edge_sum = summing(at, plans[0], acc_e, full_e, rbuf, sems, rsems)
    vec_sum = summing(at, plans[3], acc_v, full_v, rbuf, sems, rsems)
    advance(edge_sum, vec_sum)
    one = jnp.concatenate([tall(snd_ref, 0, cblocks), tall(rcv_ref, 0, cblocks)], axis=0)
    picked = split(halves(mul(one, dpre_hl[...])))
    up_s[:cells, :] = picked[:cells]
    recv_s[...] = picked[cells:]
    acc_t[0:128, :] = mul_t(table[...], up_s[...]) * scale
    acc_t[128:256, :] = mul_t(table[:cells, :], recv_s[...]) * scale
    table_sum = summing(at, plans[1], acc_t, full_t, rbuf, sems, rsems)
    advance(table_sum, edge_sum, vec_sum, node_sum)
    own_ref[...] += halves(mul(up_s[:cells, :], wst) + mul(recv_s[...], dense(w_r.T)))
    advance(table_sum)
    halo_wait(spot, slot_out, slot_in, send2, recv2)
    back = jnp.concatenate(
        [split(slot_in[...].reshape(27 * slots, LANES)), jnp.zeros((halo - 27 * slots, 2 * LANES), BF16)], axis=0
    )
    one = jnp.concatenate([pick_cols(rows_ref, t, halo // LANES) for t in range(cblocks)], axis=0)
    own_ref[...] += halves(mul(one, back))
    for _ in range(2 * len(plans[0])):
        advance(table_sum, edge_sum, vec_sum, node_sum)
    tot_e_ref[0:128, :] = full_e[0:128, :]
    tot_e_ref[128:384, :] = full_t[...]
    tot_o_ref[...] = full_e[128:256, :]
    tot_n_ref[...] = full_n[0:256, :]
    tot_m_ref[...] = full_n[256:384, :]
    for i, ref in enumerate((tot_ebias_ref, tot_egain_ref, tot_nbias_ref, tot_ngain_ref)):
        ref[...] = full_v[i : i + 1, :]
    out_copy.wait()


def finish_kernel(*refs):
    count = (len(refs) - 1) // 2
    sems = refs[-1]
    copies = []
    for src, dst in zip(refs[:count], refs[count : 2 * count]):
        rows = src.shape[0]
        step = max(rows // 4, 256) if rows > 256 else rows
        for low in range(0, rows, step):
            part = pl.ds(low, min(step, rows - low))
            copies.append(pltpu.make_async_copy(src.at[part], dst.at[part], sems.at[len(copies)]))
    for copy in copies:
        copy.start()
    for copy in copies:
        copy.wait()


def on_device(
    node_feat, edge_feat, node_cot, edge_cot, sender, receiver, block_count, send_rows,
    edge_in_weight, edge_bias, edge_out_weight, edge_gain,
    node_in_weight, node_bias, node_out_weight, node_gain,
):
    cells, width = node_feat.shape
    edges = edge_feat.shape[0]
    slots = send_rows.shape[3]
    total = lax.axis_size("gx") * lax.axis_size("gy") * lax.axis_size("gz") * edges
    scale = 1.0 / math.sqrt(total)
    halo = -(-27 * slots // LANES) * LANES
    rows = jnp.where((jnp.arange(27) != 13)[:, None], send_rows.reshape(27, slots), -1).reshape(27 * slots)
    rows = jnp.pad(rows, (0, halo - 27 * slots), constant_values=-1).reshape(halo // LANES, LANES)

    sizes = tuple(lax.axis_size(axis) for axis in AXES)
    tbl = cells + halo
    plan_e, slot, sem = sum_plan(sizes, 256, 0, 0)
    plan_t, slot, sem = sum_plan(sizes, 256, slot, sem)
    plan_n, slot, sem = sum_plan(sizes, 384, slot, sem)
    plan_v, slot, sem = sum_plan(sizes, 8, slot, sem)
    link = [pltpu.VMEM((27, slots, width), F32)] * 4
    dma = lambda n: pltpu.SemaphoreType.DMA((n,))
    big = lambda dtype, cols: pltpu.VMEM((edges, cols), dtype)
    keep = lambda r: pltpu.VMEM((r, width), F32)
    pair = lambda r: pltpu.VMEM((r, 2 * width), BF16)
    hbm = pl.BlockSpec(memory_space=pl.ANY)
    square = lambda r: jax.ShapeDtypeStruct((r, width), F32)
    outs = (square(cells), square(edges), square(384), square(128), square(256), square(128)) + (square(1),) * 4
    made = pl.pallas_call(
        functools.partial(fused_kernel, sizes, (plan_e, plan_t, plan_n, plan_v), scale),
        out_shape=outs,
        in_specs=[VMEM, hbm, hbm, hbm, VMEM, VMEM, pl.BlockSpec(memory_space=pltpu.SMEM), VMEM] + [VMEM] * 8,
        out_specs=(VMEM, hbm) + (VMEM,) * 8,
        scratch_shapes=[
            pair(tbl), pair(tbl + cells), keep(edges), keep(cells), keep(edges), keep(edges),
            pair(edges), pair(edges), keep(edges), keep(edges), keep(edges),
            pair(edges), pair(edges), pair(edges), pair(tbl), pair(cells),
            keep(256), keep(256), keep(384), keep(8), keep(256), keep(256), keep(384), keep(8), keep(slot),
        ]
        + link
        + [dma(3), dma(1), dma(27), dma(27), dma(27), dma(27), dma(sem), dma(sem)],
        compiler_params=pltpu.CompilerParams(
            collective_id=0, has_side_effects=True, vmem_limit_bytes=56 * 1024 * 1024
        ),
        name="layer",
    )(
        node_feat, edge_feat, node_cot, edge_cot,
        sender.reshape(edges // LANES, LANES), receiver.reshape(edges // LANES, LANES), block_count, rows,
        edge_in_weight, edge_bias.reshape(1, width), edge_out_weight, edge_gain.reshape(1, width),
        node_in_weight, node_bias.reshape(1, width), node_out_weight, node_gain.reshape(1, width),
    )
    node_grad, edge_grad, ein, eout, nin, nout, ebias, egain, nbias, ngain = pl.pallas_call(
        finish_kernel,
        out_shape=outs,
        in_specs=[hbm] * len(outs),
        out_specs=(hbm,) * len(outs),
        scratch_shapes=[dma(24)],
        name="finish",
    )(*made)
    flat = lambda x: x.reshape(width)
    return (node_grad, edge_grad, ein, flat(ebias), eout, flat(egain), nin, flat(nbias), nout, flat(ngain))


def solution(mesh):
    part = P(AXES, None)
    flat = P(AXES)
    return jax.shard_map(
        on_device,
        mesh=mesh,
        in_specs=(part,) * 4 + (flat,) * 3 + (P("gx", "gy", "gz", None),) + (P(),) * 8,
        out_specs=(part,) * 2 + (P(),) * 8,
        check_vma=False,
    )
```

```python
import functools
import math

import jax
import jax.numpy as jnp
from jax import lax
from jax.experimental import pallas as pl
from jax.experimental.pallas import tpu as pltpu
from jax.sharding import PartitionSpec as P

NORM_EPS = 1e-05
LANES = 128
CHUNK = 512
AXES = ("gx", "gy", "gz")
F32, BF16 = jnp.float32, jnp.bfloat16
VMEM = pl.BlockSpec(memory_space=pltpu.VMEM)


def split(x):
    high = x.astype(BF16)
    low = (x - high.astype(F32)).astype(BF16)
    return jnp.concatenate([high, low], axis=1)


def dense(w):
    row = split(w)
    return jnp.concatenate([row, row], axis=0)


def halves(y):
    return y[:, :LANES] + y[:, LANES:]


def mul(a, b):
    return jnp.dot(a, b, preferred_element_type=F32)


def mul_t(a, b):
    y = lax.dot_general(a, b, (((0,), (0,)), ((), ())), preferred_element_type=F32)
    return halves(y[:LANES] + y[LANES:])


def hot(mask):
    return jnp.where(mask, 1.0, 0.0).astype(BF16)


def pick_rows(idx_row, blocks):
    col = jnp.broadcast_to(idx_row, (LANES, LANES)).T
    lane = lax.broadcasted_iota(jnp.int32, (LANES, LANES), 1)
    return jnp.concatenate([hot(col == lane + LANES * k) for k in range(blocks)], axis=1)


def pick_cols(idx_ref, tile, blocks):
    row = lax.broadcasted_iota(jnp.int32, (LANES, LANES), 0) + LANES * tile
    return jnp.concatenate(
        [hot(jnp.broadcast_to(idx_ref[b : b + 1, :], (LANES, LANES)) == row) for b in range(blocks)],
        axis=1,
    )


def centre(x):
    return x - jnp.mean(x, axis=-1, keepdims=True)


def position(sizes):
    return tuple(lax.axis_index(axis) for axis in AXES), sizes


def directions(spot):
    at, sizes = spot
    for d in range(27):
        if d == 13:
            continue
        step = (d // 9 - 1, d // 3 % 3 - 1, d % 3 - 1)
        if any(n == 1 and s != 0 for n, s in zip(sizes, step)):
            continue
        inside = None
        for p, n, s in zip(at, sizes, step):
            if s:
                ok = p > 0 if s < 0 else p < n - 1
                inside = ok if inside is None else jnp.logical_and(inside, ok)
        yield d, inside, tuple(p + s for p, s in zip(at, step))


def greet_neighbours(spot, barrier):
    for _, inside, where in directions(spot):

        @pl.when(inside)
        def _():
            pl.semaphore_signal(barrier, inc=1, device_id=where, device_id_type=pl.DeviceIdType.MESH)

    count = 1
    for p, n in zip(*spot):
        count = count * (1 + (p > 0).astype(jnp.int32) + (p < n - 1).astype(jnp.int32))
    return count - 1


def halo_copy(d, where, out, land, send, recv):
    return pltpu.make_async_remote_copy(
        src_ref=out.at[d], dst_ref=land.at[26 - d], send_sem=send.at[d], recv_sem=recv.at[26 - d],
        device_id=where, device_id_type=pl.DeviceIdType.MESH,
    )


def halo_start(spot, out, land, send, recv):
    for d, inside, where in directions(spot):

        @pl.when(inside)
        def _():
            halo_copy(d, where, out, land, send, recv).start()


def halo_wait(spot, out, land, send, recv):
    for d, inside, where in directions(spot):

        @pl.when(inside)
        def _():
            halo_copy(d, where, out, land, send, recv).wait_send()
            halo_copy(26 - d, where, out, land, send, recv).wait_recv()


def sum_plan(sizes, rows, slot, sem):
    bits = []
    for axis in (1, 0, 2):
        stride = 1
        while stride < sizes[axis]:
            bits.append((axis, stride))
            stride *= 2
    groups = [bits[:1]] + [bits[i : i + 2] for i in range(1, len(bits), 2)]
    steps, r = [], rows
    for group in groups:
        n = 2 ** len(group)
        scatters = r > 64 and r % (8 * n) == 0
        r = r // n if scatters else r
        steps.append((tuple(group), scatters, r, slot, sem))
        slot, sem = slot + (n - 1) * r, sem + 2 * (n - 1)
    return steps, slot, sem


def peers_of(at, group):
    own = [lax.rem(at[axis] // stride, 2) for axis, stride in group]
    digit = sum(b * 2**i for i, b in enumerate(own))
    others = []
    for k in range(1, 2 ** len(group)):
        where, other = list(at), 0
        for i, (axis, stride) in enumerate(group):
            bit = own[i]
            if k >> i & 1:
                where[axis] = where[axis] + (1 - 2 * bit) * stride
                bit = 1 - bit
            other = other + bit * 2**i
        others.append((k, other, tuple(where)))
    return digit, others


def summing(at, steps, acc, full, rbuf, sems, rsems):
    def block(ref, start, r):
        return ref.at[pl.ds(pl.multiple_of(start, 8), r)]

    def remote(src, dst, sem, where):
        return pltpu.make_async_remote_copy(
            src_ref=src, dst_ref=dst, send_sem=sems.at[sem], recv_sem=rsems.at[sem],
            device_id=where, device_id_type=pl.DeviceIdType.MESH,
        )

    off = 0
    for group, scatters, r, slot, sem in steps:
        digit, others = peers_of(at, group)
        copies = [
            remote(
                block(acc, off + other * r if scatters else off, r),
                rbuf.at[pl.ds(slot + (k - 1) * r, r)], sem + k - 1, where,
            )
            for k, other, where in others
        ]
        for copy in copies:
            copy.start()
        yield
        for copy in copies:
            copy.wait()
        off = off + digit * r if scatters else off
        here = pl.ds(pl.multiple_of(off, 8), r)
        terms = [acc[here, :]] + [rbuf[slot + k * r : slot + (k + 1) * r, :] for k in range(len(others))]
        while len(terms) > 1:
            terms = [terms[i] + terms[i + 1] for i in range(0, len(terms), 2)]
        acc[here, :] = terms[0]
    last = steps[-1][2]
    here = pl.ds(pl.multiple_of(off, 8), last)
    full[here, :] = acc[here, :]
    for group, scatters, r, slot, sem in reversed(steps):
        if not scatters:
            continue
        digit, others = peers_of(at, group)
        base = off - digit * r
        first = sem + len(others) - 1
        for k, other, where in others:
            remote(block(full, off, r), block(full, off, r), first + k, where).start()
        yield
        for k, other, where in others:
            remote(block(full, off, r), block(full, off, r), first + k, where).wait_send()
            came = block(full, base + other * r, r)
            remote(came, came, first + k, where).wait_recv()
        off = base


def advance(*sums):
    for one in sums:
        next(one, None)


def fused_kernel(
    sizes, plans, scale,
    feat_ref, edge_ref, ncot_ref, ecot_ref, snd_ref, rcv_ref, cnt_ref, rows_ref,
    ein_ref, ebias_ref, eout_ref, egain_ref, nin_ref, nbias_ref, nout_ref, ngain_ref,
    own_ref, egrad_ref, tot_e_ref, tot_o_ref, tot_n_ref, tot_m_ref,
    tot_ebias_ref, tot_egain_ref, tot_nbias_ref, tot_ngain_ref,
    table, both, edge_f, ncot_f, ecot_f, egrad_f, edge_hl, hid_hl, dsilu_s, xhat_s, rstd_s,
    msg_hl, dout_hl, dpre_hl, up_s, recv_s,
    acc_e, acc_t, acc_n, acc_v, full_e, full_t, full_n, full_v, rbuf,
    packets, land, slot_out, slot_in,
    load, store, send, recv, send2, recv2, sems, rsems,
):
    spot = position(sizes)
    at = spot[0]
    cells, edges = feat_ref.shape[0], edge_ref.shape[0]
    slots = packets.shape[1]
    halo = rows_ref.shape[0] * LANES
    tbl = cells + halo
    sub = CHUNK // LANES
    eblocks, cblocks = edges // LANES, cells // LANES
    chunks = edges // CHUNK

    loads = [
        pltpu.make_async_copy(src, dst, load.at[i])
        for i, (src, dst) in enumerate(((edge_ref, edge_f), (ncot_ref, ncot_f), (ecot_ref, ecot_f)))
    ]
    for copy in loads:
        copy.start()
    land[...] = jnp.zeros_like(land)
    slot_in[...] = jnp.zeros_like(slot_in)
    barrier = pltpu.get_barrier_semaphore()
    count = greet_neighbours(spot, barrier)
    for step in plans[0]:
        for _, _, where in peers_of(at, step[0])[1]:
            pl.semaphore_signal(barrier, inc=1, device_id=where, device_id_type=pl.DeviceIdType.MESH)
            count = count + 1

    table[:cells, :] = split(feat_ref[...])
    per = LANES // slots
    for b in range(rows_ref.shape[0]):
        picked = halves(mul(pick_rows(rows_ref[b : b + 1, :], cblocks), table[:cells, :]))
        for k in range(per):
            if b * per + k < 27:
                packets[b * per + k] = picked[k * slots : (k + 1) * slots]
    pl.semaphore_wait(barrier, count)
    halo_start(spot, packets, land, send, recv)

    ein = ein_ref[...]
    w_e, w_s, w_r = ein[:LANES], ein[LANES : 2 * LANES], ein[2 * LANES :]
    eoc = centre(eout_ref[...])
    gain, bias = egain_ref[...], ebias_ref[...]
    ws_cat, we_cat, wo_cat = dense(w_s), dense(w_e), dense(eoc)
    both[:cells, :] = split(halves(mul(table[:cells, :], ws_cat)))
    both[cells : 2 * cells, :] = split(halves(mul(table[:cells, :], dense(w_r))))
    loads[0].wait()

    def valid_of(c):
        row = lax.broadcasted_iota(jnp.int32, (LANES, LANES), 0)
        return jnp.concatenate([jnp.where(row < cnt_ref[c * sub + k], 1.0, 0.0) for k in range(sub)], axis=0)

    def picks(ref, c, low, blocks):
        return jnp.concatenate(
            [pick_rows(ref[pl.ds(c * sub + k, 1), :] - low, blocks) for k in range(sub)], axis=0
        )

    def before(c, carry):
        here = pl.ds(pl.multiple_of(c * CHUNK, CHUNK), CHUNK)
        one = jnp.concatenate([picks(snd_ref, c, 0, cblocks), picks(rcv_ref, c, 0, cblocks)], axis=1)
        feat = split(edge_f[here, :])
        edge_hl[here, :] = feat
        dsilu_s[here, :] = halves(mul(one, both[: 2 * cells, :]) + mul(feat, we_cat)) + bias
        return carry

    lax.fori_loop(0, chunks, before, 0)

    halo_wait(spot, packets, land, send, recv)
    table[cells : cells + 27 * slots, :] = split(land[...].reshape(27 * slots, LANES))
    table[cells + 27 * slots :, :] = jnp.zeros((halo - 27 * slots, 2 * LANES), BF16)
    both[2 * cells :, :] = split(halves(mul(table[cells:, :], ws_cat)))

    def forward(c, carry):
        here = pl.ds(pl.multiple_of(c * CHUNK, CHUNK), CHUNK)
        one = picks(snd_ref, c, cells, halo // LANES)
        pre = dsilu_s[here, :] + halves(mul(one, both[2 * cells :, :]))
        sig = jax.nn.sigmoid(pre)
        hid = pre * sig
        dsilu_s[here, :] = sig + hid * (1.0 - sig)
        hid = split(hid)
        hid_hl[here, :] = hid
        out = halves(mul(hid, wo_cat))
        rstd = lax.rsqrt(jnp.mean(out * out, axis=-1, keepdims=True) + NORM_EPS)
        xhat = out * rstd
        rstd_s[here, :] = jnp.broadcast_to(rstd, out.shape)
        xhat_s[here, :] = xhat
        msg_hl[here, :] = split(xhat * gain * valid_of(c))
        return carry

    lax.fori_loop(0, chunks, forward, 0)

    summed = jnp.concatenate(
        [halves(mul(pick_cols(rcv_ref, t, eblocks), msg_hl[...])) for t in range(cblocks)], axis=0
    )
    nin, ngain = nin_ref[...], ngain_ref[...]
    noc = centre(nout_ref[...])
    feat_hl, sum_hl = table[:cells, :], split(summed)
    pre = halves(mul(feat_hl, dense(nin[:LANES])) + mul(sum_hl, dense(nin[LANES:]))) + nbias_ref[...]
    sig = jax.nn.sigmoid(pre)
    hid = pre * sig
    dsilu = sig + hid * (1.0 - sig)
    hid = split(hid)
    out = halves(mul(hid, dense(noc)))
    rstd = lax.rsqrt(jnp.mean(out * out, axis=-1, keepdims=True) + NORM_EPS)
    xhat = out * rstd
    loads[1].wait()
    ncot = ncot_f[...]
    dn = ncot * ngain
    dout = split(rstd * (dn - xhat * jnp.mean(dn * xhat, axis=-1, keepdims=True)))
    dpre = halves(mul(dout, dense(noc.T))) * dsilu
    dpre_n = split(dpre)
    dsum = split(halves(mul(dpre_n, dense(nin[LANES:].T))))
    acc_n[0:128, :] = mul_t(feat_hl, dpre_n) * scale
    acc_n[128:256, :] = mul_t(sum_hl, dpre_n) * scale
    acc_n[256:384, :] = centre(mul_t(hid, dout)) * scale
    node_sum = summing(at, plans[2], acc_n, full_n, rbuf, sems, rsems)
    advance(node_sum)
    own_ref[...] = ncot + halves(mul(dpre_n, dense(nin[:LANES].T)))
    nbias_g = jnp.sum(dpre, axis=0, keepdims=True)
    ngain_g = jnp.sum(ncot * xhat, axis=0, keepdims=True)

    wot_cat, wet_cat = dense(eoc.T), dense(w_e.T)
    loads[2].wait()

    def backward(c, carry):
        bias_g, gain_g = carry
        here = pl.ds(pl.multiple_of(c * CHUNK, CHUNK), CHUNK)
        ecot = ecot_f[here, :]
        xhat = xhat_s[here, :]
        dm = (ecot + halves(mul(picks(rcv_ref, c, 0, cblocks), dsum))) * valid_of(c)
        dn = dm * gain
        dout = split(rstd_s[here, :] * (dn - xhat * jnp.mean(dn * xhat, axis=-1, keepdims=True)))
        dout_hl[here, :] = dout
        dpre = halves(mul(dout, wot_cat)) * dsilu_s[here, :]
        dpre_c = split(dpre)
        dpre_hl[here, :] = dpre_c
        egrad_f[here, :] = ecot + halves(mul(dpre_c, wet_cat))
        fold = lambda x: jnp.sum(x.reshape(CHUNK // 8, 8, LANES), axis=0)
        return bias_g + fold(dpre), gain_g + fold(dm * xhat)

    zero = jnp.zeros((8, LANES), F32)
    sums = lax.fori_loop(0, chunks // 2, backward, (zero, zero))
    advance(node_sum)
    ebias_g, egain_g = lax.fori_loop(chunks // 2, chunks, backward, sums)
    advance(node_sum)
    out_copy = pltpu.make_async_copy(egrad_f, egrad_ref, store.at[0])
    out_copy.start()

    wst = dense(w_s.T)

    def up(t, carry):
        out = pl.ds(pl.multiple_of(t * LANES, LANES), LANES)
        up_s[out, :] = split(halves(mul(pick_cols(snd_ref, t, eblocks), dpre_hl[...])))
        return carry

    def down(t, carry):
        out = pl.ds(pl.multiple_of(t * LANES, LANES), LANES)
        recv_s[out, :] = split(halves(mul(pick_cols(rcv_ref, t, eblocks), dpre_hl[...])))
        return carry

    lax.fori_loop(cblocks, tbl // LANES, up, 0)
    slot_out[...] = halves(mul(up_s[cells : cells + 27 * slots, :], wst)).reshape(27, slots, LANES)
    halo_start(spot, slot_out, slot_in, send2, recv2)
    advance(node_sum)
    acc_e[0:128, :] = mul_t(edge_hl[...], dpre_hl[...]) * scale
    acc_e[128:256, :] = centre(mul_t(hid_hl[...], dout_hl[...])) * scale
    acc_v[...] = jnp.concatenate(
        [
            jnp.sum(ebias_g, axis=0, keepdims=True),
            jnp.sum(egain_g, axis=0, keepdims=True),
            nbias_g,
            ngain_g,
            jnp.zeros((4, LANES), F32),
        ],
        axis=0,
    ) * scale
    edge_sum = summing(at, plans[0], acc_e, full_e, rbuf, sems, rsems)
    vec_sum = summing(at, plans[3], acc_v, full_v, rbuf, sems, rsems)
    advance(edge_sum, vec_sum)
    lax.fori_loop(0, cblocks, up, 0)
    advance(edge_sum, vec_sum, node_sum)
    lax.fori_loop(0, cblocks, down, 0)
    acc_t[0:128, :] = mul_t(table[...], up_s[...]) * scale
    acc_t[128:256, :] = mul_t(table[:cells, :], recv_s[...]) * scale
    table_sum = summing(at, plans[1], acc_t, full_t, rbuf, sems, rsems)
    advance(table_sum, edge_sum, vec_sum, node_sum)
    own_ref[...] += halves(mul(up_s[:cells, :], wst) + mul(recv_s[...], dense(w_r.T)))
    advance(table_sum)
    halo_wait(spot, slot_out, slot_in, send2, recv2)
    back = jnp.concatenate(
        [split(slot_in[...].reshape(27 * slots, LANES)), jnp.zeros((halo - 27 * slots, 2 * LANES), BF16)], axis=0
    )
    one = jnp.concatenate([pick_cols(rows_ref, t, halo // LANES) for t in range(cblocks)], axis=0)
    own_ref[...] += halves(mul(one, back))
    for _ in range(2 * len(plans[0])):
        advance(table_sum, edge_sum, vec_sum, node_sum)
    tot_e_ref[0:128, :] = full_e[0:128, :]
    tot_e_ref[128:384, :] = full_t[...]
    tot_o_ref[...] = full_e[128:256, :]
    tot_n_ref[...] = full_n[0:256, :]
    tot_m_ref[...] = full_n[256:384, :]
    for i, ref in enumerate((tot_ebias_ref, tot_egain_ref, tot_nbias_ref, tot_ngain_ref)):
        ref[...] = full_v[i : i + 1, :]
    out_copy.wait()


def finish_kernel(*refs):
    count = len(refs) // 2
    for src, dst in zip(refs[:count], refs[count:]):
        dst[...] = src[...]


def on_device(
    node_feat, edge_feat, node_cot, edge_cot, sender, receiver, block_count, send_rows,
    edge_in_weight, edge_bias, edge_out_weight, edge_gain,
    node_in_weight, node_bias, node_out_weight, node_gain,
):
    cells, width = node_feat.shape
    edges = edge_feat.shape[0]
    slots = send_rows.shape[3]
    total = lax.axis_size("gx") * lax.axis_size("gy") * lax.axis_size("gz") * edges
    scale = 1.0 / math.sqrt(total)
    halo = -(-27 * slots // LANES) * LANES
    rows = jnp.where((jnp.arange(27) != 13)[:, None], send_rows.reshape(27, slots), -1).reshape(27 * slots)
    rows = jnp.pad(rows, (0, halo - 27 * slots), constant_values=-1).reshape(halo // LANES, LANES)

    sizes = tuple(lax.axis_size(axis) for axis in AXES)
    tbl = cells + halo
    plan_e, slot, sem = sum_plan(sizes, 256, 0, 0)
    plan_t, slot, sem = sum_plan(sizes, 256, slot, sem)
    plan_n, slot, sem = sum_plan(sizes, 384, slot, sem)
    plan_v, slot, sem = sum_plan(sizes, 8, slot, sem)
    link = [pltpu.VMEM((27, slots, width), F32)] * 4
    dma = lambda n: pltpu.SemaphoreType.DMA((n,))
    big = lambda dtype, cols: pltpu.VMEM((edges, cols), dtype)
    keep = lambda r: pltpu.VMEM((r, width), F32)
    pair = lambda r: pltpu.VMEM((r, 2 * width), BF16)
    hbm = pl.BlockSpec(memory_space=pl.ANY)
    square = lambda r: jax.ShapeDtypeStruct((r, width), F32)
    outs = (square(cells), square(edges), square(384), square(128), square(256), square(128)) + (square(1),) * 4
    made = pl.pallas_call(
        functools.partial(fused_kernel, sizes, (plan_e, plan_t, plan_n, plan_v), scale),
        out_shape=outs,
        in_specs=[VMEM, hbm, hbm, hbm, VMEM, VMEM, pl.BlockSpec(memory_space=pltpu.SMEM), VMEM] + [VMEM] * 8,
        out_specs=(VMEM, hbm) + (VMEM,) * 8,
        scratch_shapes=[
            pair(tbl), pair(tbl + cells), keep(edges), keep(cells), keep(edges), keep(edges),
            pair(edges), pair(edges), keep(edges), keep(edges), keep(edges),
            pair(edges), pair(edges), pair(edges), pair(tbl), pair(cells),
            keep(256), keep(256), keep(384), keep(8), keep(256), keep(256), keep(384), keep(8), keep(slot),
        ]
        + link
        + [dma(3), dma(1), dma(27), dma(27), dma(27), dma(27), dma(sem), dma(sem)],
        compiler_params=pltpu.CompilerParams(
            collective_id=0, has_side_effects=True, vmem_limit_bytes=56 * 1024 * 1024
        ),
        name="layer",
    )(
        node_feat, edge_feat, node_cot, edge_cot,
        sender.reshape(edges // LANES, LANES), receiver.reshape(edges // LANES, LANES), block_count, rows,
        edge_in_weight, edge_bias.reshape(1, width), edge_out_weight, edge_gain.reshape(1, width),
        node_in_weight, node_bias.reshape(1, width), node_out_weight, node_gain.reshape(1, width),
    )
    node_grad, edge_grad, ein, eout, nin, nout, ebias, egain, nbias, ngain = pl.pallas_call(
        finish_kernel,
        out_shape=outs,
        in_specs=[VMEM] * len(outs),
        out_specs=(VMEM,) * len(outs),
        name="finish",
    )(*made)
    flat = lambda x: x.reshape(width)
    return (node_grad, edge_grad, ein, flat(ebias), eout, flat(egain), nin, flat(nbias), nout, flat(ngain))


def solution(mesh):
    part = P(AXES, None)
    flat = P(AXES)
    return jax.shard_map(
        on_device,
        mesh=mesh,
        in_specs=(part,) * 4 + (flat,) * 3 + (P("gx", "gy", "gz", None),) + (P(),) * 8,
        out_specs=(part,) * 2 + (P(),) * 8,
        check_vma=False,
    )
```
